256 devices in a mesh: occ: 128 (over x_lo, z, y, core), aux: 2 (over x_hi).
Axes of the slice: x: 4 (x_hi: 2, x_lo: 2; x = x_hi * 2 + x_lo), y: 4, z: 8, core: 2. Of those that a mesh axis runs over, the one named last changes fastest.
Arguments:
- cholesky: bfloat16 [128, 5120, 1024], P('occ', 'aux'), may hold values from -0.099609375 to 0.099609375
- occ_energy: float32 [128], replicated, may hold values from -1.5 to -0.4
- vir_energy: float32 [1024], replicated, may hold values from 0.3 to 4
Outputs:
- vir_density: float32 [1024, 1024], P('occ', 'aux')
- occ_diagonal: float32 [128], P('occ')
The draws below stay inside these ranges and needn't reach their ends.
All inputs are finite; a program needn't handle non-finite values.
Results may differ from the reference program's by a relative error of at most 0.0044.
Values may be sent and summed in bfloat16 or wider, within the bound.
A program may use at most 64 MiB of HBM per device.

```python
import math
import jax
import jax.numpy as jnp
from jax import lax

NAUX = 5120
NVIR = 1024
STEPS = 2
NOCC = 128


def levels(own_key, dims, pieces, least, largest):
    gain = 1.0
    for dim, shards_of in pieces:
        heights = jax.random.uniform(jax.random.fold_in(jax.random.fold_in(own_key, 6), dim), (shards_of,), jnp.float32, least / len(pieces), largest / len(pieces))
        gain = gain * jnp.repeat(jnp.exp(heights), dims[dim] // shards_of).reshape((-1,) + (1,) * (len(dims) - 1 - dim))
    return gain


def centred(own_key, extent, spread, bound, pieces=(), held_as=jnp.bfloat16):
    factor_of = levels(own_key, extent, pieces, -0.22, 0.18) if pieces else 1.0
    drawn = jax.random.normal(own_key, extent, jnp.float32) * spread * factor_of
    return jnp.minimum(jnp.maximum(drawn, -bound), bound).astype(held_as)


def setup_inputs(seed: int = 0) -> dict:
    keys = jax.random.split(jax.random.key(seed), 4)
    return {
        "cholesky": centred(keys[0], (NOCC, NAUX, NVIR), 0.018, 0.099609375, ((0, 128), (1, 2))),
        "occ_energy": jnp.clip(jax.random.uniform(keys[1], (NOCC,), jnp.float32, -1.5, -0.4), -1.5, -0.4),
        "vir_energy": jnp.clip(jnp.exp(jax.random.uniform(keys[2], (NVIR,), jnp.float32, math.log(0.3), math.log(4.0))), 0.3, 4.0),
    }


def reference(cholesky, occ_energy, vir_energy):
    number = cholesky.shape[0]
    pair_sum = vir_energy[:, None] + vir_energy[None, :]

    def visit(density, center):
        left_block = lax.dynamic_index_in_dim(cholesky, center, 0, keepdims=False)
        center_energy = lax.dynamic_index_in_dim(occ_energy, center, 0, keepdims=False)
        totals = []
        for offset in range(1, STEPS + 1):
            partner = ((center + offset) % number).astype(jnp.int32)
            right_block = lax.dynamic_index_in_dim(cholesky, partner, 0, keepdims=False)
            partner_energy = lax.dynamic_index_in_dim(occ_energy, partner, 0, keepdims=False)
            integrals = lax.dot_general(left_block, right_block, (((0,), (0,)), ((), ())), preferred_element_type=jnp.float32)
            amplitude = (integrals / (pair_sum - center_energy - partner_energy)).astype(jnp.bfloat16)
            wide = amplitude.astype(jnp.float32)
            tilde = (2.0 * wide - wide.T).astype(jnp.bfloat16)
            density = density + 2.0 * lax.dot_general(amplitude, tilde, (((1,), (1,)), ((), ())), preferred_element_type=jnp.float32)
            totals.append(-(2.0 / NVIR) * jnp.sum(wide * tilde.astype(jnp.float32)))
        return density, jnp.stack(totals)

    density, band = lax.scan(visit, jnp.zeros((NVIR, NVIR), jnp.float32), jnp.arange(number, dtype=jnp.int32))
    diagonal = jnp.zeros((number,), jnp.float32)
    for offset in range(1, STEPS + 1):
        diagonal = diagonal + jnp.roll(band[:, offset - 1], offset)
    return density, diagonal
```

```python
import functools

import jax
import jax.numpy as jnp
from jax import lax
from jax.experimental import pallas as pl
from jax.experimental.pallas import tpu as pltpu
from jax.sharding import PartitionSpec as P

MESH = pl.DeviceIdType.MESH
NAUX_HALF = 2560
NVIR = 1024
NOCC = 128
NC = 8
CW = NVIR // NC
HALF = NVIR // 2
f32 = jnp.float32
bf16 = jnp.bfloat16


def kernel(
    x_ref, eocc_ref, v_ref, dens_ref, diag_ref,
    own, own_t, blocks, sendb, recvb, acc, lr, tt, dens, dens_in, sx, rx, fsum, ry, gsum, rz, tbuf, colv,
    own_sem, ys, yr, ds, dr, xs, xr, cs, cr, qs, qr, us, ur, zs, zr, ts, tr,
):
    k = lax.axis_index("occ")
    h = lax.axis_index("aux")
    core = lax.rem(k, 2)
    y = lax.rem(k // 2, 4)
    z = lax.rem(k // 8, 8)
    x = h * 2 + k // 64
    inner = lax.rem(k, 64)

    def x_place(d):
        to = lax.rem(x + d, 4)
        return {"occ": lax.rem(to, 2) * 64 + inner, "aux": to // 2}

    def y_place(d):
        return {"occ": k + (lax.rem(y + d, 4) - y) * 2, "aux": h}

    def z_place(d):
        return {"occ": k + (lax.rem(z + d, 8) - z) * 8, "aux": h}

    above = {"occ": lax.rem(k + 2, NOCC), "aux": h}
    below = {"occ": lax.rem(k + NOCC - 2, NOCC), "aux": h}
    sibling = {"occ": k + 1 - 2 * core, "aux": h}
    partner = {"occ": k, "aux": 1 - h}
    onward = {"occ": lax.rem(k + NOCC - 2 + 4 * core, NOCC), "aux": h}

    def remote(src, dst, send, recv, device):
        return pltpu.make_async_remote_copy(
            src_ref=src, dst_ref=dst, send_sem=send, recv_sem=recv, device_id=device, device_id_type=MESH
        )

    load = pltpu.make_async_copy(x_ref.at[0], own, own_sem)
    load.start()

    barrier = pltpu.get_barrier_semaphore()
    greeted = [above, below, sibling, partner, x_place(1), x_place(3)]
    greeted += [y_place(d) for d in range(1, 4)] + [z_place(d) for d in range(1, 8)]
    for device in greeted:
        pl.semaphore_signal(barrier, inc=1, device_id=device, device_id_type=MESH)
    pl.semaphore_wait(barrier, len(greeted))

    def columns(j):
        return pl.ds(pl.multiple_of(j * CW, CW), CW)

    def ring_copy(j):
        return remote(x_ref.at[0, :, columns(j)], blocks.at[0, j], ys.at[j], yr.at[j], onward)

    def own_copy(j):
        return remote(x_ref.at[0, :, columns(j)], blocks.at[1, j], ds.at[j], dr.at[j], sibling)

    def pass_copy(j):
        return remote(blocks.at[0, j], blocks.at[1, j], ds.at[j], dr.at[j], sibling)

    def pair_copy(j):
        return remote(sendb.at[j], recvb.at[j], xs.at[j], xr.at[j], partner)

    @pl.loop(0, NC)
    def _(j):
        ring_copy(j).start()

        @pl.when(core == 0)
        def _():
            own_copy(j).start()

    for m in range(8):
        row = v_ref[0:1, m * 128:(m + 1) * 128]
        colv[m * 128:(m + 1) * 128, :] = jnp.broadcast_to(row, (128, 128)).T

    load.wait()

    @pl.loop(0, NAUX_HALF // 128)
    def _(i):
        rows = pl.ds(pl.multiple_of(i * 128, 128), 128)
        own_t[:, rows] = own[rows, :].T

    center = lax.rem(k - h - 2 * core * (1 - h) + NOCC, NOCC)
    other = lax.rem(center + 2 - h, NOCC)
    center_energy = eocc_ref[center]
    other_energy = eocc_ref[other]
    place = 1 - (1 - core) * (1 - h)

    def finish(j):
        pair_copy(j).wait_recv()
        vrow = v_ref[0:1, columns(j)]

        @pl.loop(0, 8)
        def _(m):
            rows = pl.ds(pl.multiple_of(m * 128, 128), 128)
            total = acc[j, rows, :] + recvb[j, rows, :].astype(f32)
            part = total / (colv[rows, :] + vrow - center_energy - other_energy)
            lr[place, rows, columns(j)] = part.astype(bf16)
            lr[1 - place, columns(j), rows] = part.T.astype(bf16)

    @pl.loop(0, NC + 1)
    def _(j):
        @pl.when(j < NC)
        def _():
            ring_copy(j).wait_recv()

            @pl.when(core == 1)
            def _():
                pass_copy(j).start()

            own_copy(j).wait_recv()
            for m in range(4):
                rows = pl.ds(m * 256, 256)
                sendb[j, rows, :] = jnp.dot(
                    own_t[rows, :], blocks[1 - h, j], preferred_element_type=f32
                ).astype(bf16)
            pair_copy(j).start()
            for m in range(4):
                rows = pl.ds(m * 256, 256)
                acc[j, rows, :] = jnp.dot(own_t[rows, :], blocks[h, j], preferred_element_type=f32)

        @pl.when(j > 0)
        def _():
            finish(j - 1)

    def tilde_rows(i, term):
        rows = pl.ds(pl.multiple_of(i * 128, 128), 128)
        left = lr[0, rows, :].astype(f32)
        right = lr[1, rows, :].astype(f32)
        tilde = (2.0 * right - left).astype(bf16)
        tt[rows, :] = tilde
        return term + jnp.sum((right * tilde.astype(f32)).reshape(16, 8, 8, 128), axis=(0, 2))

    term = lax.fori_loop(0, 8, tilde_rows, jnp.zeros((8, 128), f32))
    tbuf[h] = jnp.full((8, 128), -(2.0 / NVIR) * jnp.sum(term), f32)
    term_copy = remote(tbuf.at[h], tbuf.at[h], ts.at[0], tr.at[0], partner)
    term_copy.start()

    @pl.loop(0, 4)
    def _(i):
        rows = pl.ds(pl.multiple_of(i * 256, 256), 256)
        out = 2.0 * jnp.dot(lr[0, rows, :], tt[...], preferred_element_type=f32)
        dens[pl.ds(i * 16, 16)] = out.reshape(16, 2, 8, NVIR)

    core_copy = remote(dens.at[:, 1 - core], dens_in, cs, cr, sibling)
    core_copy.start()
    core_copy.wait_recv()

    x_copies = []
    for d in (2, 1, 3, 0):
        to = lax.rem(x + d, 4)
        groups = pl.ds(lax.rem(to, 2) * 32, 32)
        cols = pl.ds(pl.multiple_of((to // 2) * HALF, HALF), HALF)
        both = dens[groups, core, :, cols] + dens_in[groups, :, cols]
        if d == 0:
            fsum[...] = both
        else:
            sx[d - 1] = both.reshape(256, HALF).astype(bf16)
            copy = remote(sx.at[d - 1], rx.at[d - 1], qs.at[d - 1], qr.at[d - 1], x_place(d))
            copy.start()
            x_copies.append(copy)

    term_copy.wait()
    step_copy = remote(tbuf.at[0], tbuf.at[2], ts.at[1], tr.at[1], above)
    step_copy.start()

    for copy in x_copies:
        copy.wait_recv()
    fsum[...] += (rx[0].astype(f32) + rx[1].astype(f32) + rx[2].astype(f32)).reshape(32, 8, HALF)

    def y_part(to):
        return fsum.reshape(8, 4, 8, HALF).at[:, to]

    y_copies = []
    for d in (2, 1, 3):
        copy = remote(y_part(lax.rem(y + d, 4)), ry.at[d - 1], us.at[d - 1], ur.at[d - 1], y_place(d))
        copy.start()
        y_copies.append(copy)
    for copy in y_copies:
        copy.wait_recv()
    gsum[...] = y_part(y)[...] + ry[0] + ry[1] + ry[2]

    z_copies = []
    for d in (4, 3, 5, 2, 6, 1, 7):
        copy = remote(gsum.at[lax.rem(z + d, 8)], rz.at[d - 1], zs.at[d - 1], zr.at[d - 1], z_place(d))
        copy.start()
        z_copies.append(copy)

    step_copy.wait_recv()
    diag_ref[...] = tbuf[1] + jnp.where(core == 0, tbuf[2], tbuf[0])

    for copy in z_copies:
        copy.wait_recv()
    total = gsum[z]
    for d in range(7):
        total = total + rz[d]
    dens_ref[...] = total

    step_copy.wait_send()
    core_copy.wait_send()
    for copy in x_copies + y_copies + z_copies:
        copy.wait_send()

    @pl.loop(0, NC)
    def _(j):
        ring_copy(j).wait_send()
        own_copy(j).wait_send()
        pair_copy(j).wait_send()


def per_device(cholesky, occ_energy, vir_energy):
    dma = pltpu.SemaphoreType.DMA
    vmem = pltpu.VMEM
    dens, diag = pl.pallas_call(
        kernel,
        out_shape=(jax.ShapeDtypeStruct((8, HALF), f32), jax.ShapeDtypeStruct((8, 128), f32)),
        in_specs=[
            pl.BlockSpec(memory_space=pl.ANY),
            pl.BlockSpec(memory_space=pltpu.SMEM),
            pl.BlockSpec(memory_space=pltpu.VMEM),
        ],
        out_specs=(pl.BlockSpec(memory_space=pltpu.VMEM), pl.BlockSpec(memory_space=pltpu.VMEM)),
        scratch_shapes=[
            vmem((NAUX_HALF, NVIR), bf16),
            vmem((NVIR, NAUX_HALF), bf16),
            vmem((2, NC, NAUX_HALF, CW), bf16),
            vmem((NC, NVIR, CW), bf16),
            vmem((NC, NVIR, CW), bf16),
            vmem((NC, NVIR, CW), f32),
            vmem((2, NVIR, NVIR), bf16),
            vmem((NVIR, NVIR), bf16),
            vmem((64, 2, 8, NVIR), f32),
            vmem((64, 8, NVIR), f32),
            vmem((3, 256, HALF), bf16),
            vmem((3, 256, HALF), bf16),
            vmem((32, 8, HALF), f32),
            vmem((3, 8, 8, HALF), f32),
            vmem((8, 8, HALF), f32),
            vmem((7, 8, HALF), f32),
            vmem((3, 8, 128), f32),
            vmem((NVIR, 128), f32),
            dma(()),
            dma((NC,)), dma((NC,)), dma((NC,)), dma((NC,)), dma((NC,)), dma((NC,)),
            dma(()), dma(()),
            dma((3,)), dma((3,)), dma((3,)), dma((3,)), dma((7,)), dma((7,)), dma((2,)), dma((2,)),
        ],
        compiler_params=pltpu.CompilerParams(
            collective_id=0, has_side_effects=True, vmem_limit_bytes=58 * 2**20
        ),
        cost_estimate=pl.CostEstimate(flops=13_000_000_000, bytes_accessed=16_000_000, transcendentals=0),
    )(cholesky, occ_energy, vir_energy.reshape(1, NVIR))
    return dens, diag[0, :1]


def solution(mesh):
    in_specs = (P("occ", "aux", None), P(), P())
    out_specs = (P("occ", "aux"), P("occ"))
    return jax.shard_map(
        per_device, mesh=mesh, in_specs=in_specs, out_specs=out_specs, check_vma=False
    )
```

```python
import functools

import jax
import jax.numpy as jnp
from jax import lax
from jax.experimental import pallas as pl
from jax.experimental.pallas import tpu as pltpu
from jax.sharding import PartitionSpec as P

MESH = pl.DeviceIdType.MESH
NAUX_HALF = 2560
NVIR = 1024
NOCC = 128
NC = 8
CW = NVIR // NC
HALF = NVIR // 2
QUARTER = NVIR // 4
f32 = jnp.float32
bf16 = jnp.bfloat16


def kernel(
    x_ref, eocc_ref, v_ref, dens_ref, diag_ref,
    own, own_t, blocks, relay, sendb, recvb, acc, lr, tt, dens, dens_in,
    first_out, first_in, second_out, second_in, xsum, ysum, gsum, rz, tbuf, colv,
    own_sem, ys, yr, ds, dr, xs, xr, ls, lw, cs, cr, fs, fr, us, ur, zs, zr, ts, tr,
):
    k = lax.axis_index("occ")
    h = lax.axis_index("aux")
    core = lax.rem(k, 2)
    y = lax.rem(k // 2, 4)
    z = lax.rem(k // 8, 8)
    x = h * 2 + k // 64
    inner = lax.rem(k, 64)

    def x_place(d):
        to = lax.rem(x + d, 4)
        return {"occ": lax.rem(to, 2) * 64 + inner, "aux": to // 2}

    def y_place(d):
        return {"occ": k + (lax.rem(y + d, 4) - y) * 2, "aux": h}

    def z_place(d):
        return {"occ": k + (lax.rem(z + d, 8) - z) * 8, "aux": h}

    above = {"occ": lax.rem(k + 2, NOCC), "aux": h}
    below = {"occ": lax.rem(k + NOCC - 2, NOCC), "aux": h}
    sibling = {"occ": k + 1 - 2 * core, "aux": h}
    partner = {"occ": k, "aux": 1 - h}
    onward = {"occ": lax.rem(k + NOCC - 2 + 4 * core, NOCC), "aux": h}

    up = core == 1
    low = k // 64
    row, level = jnp.where(up, y, 3 - y), jnp.where(up, z, 7 - z)

    def corner_place(low, row, level):
        inner = jnp.where(up, level * 8 + row * 2, (7 - level) * 8 + (3 - row) * 2) + core
        return {"occ": low * 64 + inner, "aux": h}

    def at(row_is, level_is):
        return (row == row_is) & (level == level_is)

    leaves, meets = at(3, 7), at(0, 0)
    early_a, early_b, late_a, late_b = at(3, 4), at(3, 5), at(3, 1), at(3, 2)
    hands_on = early_a | early_b
    hands_in = meets | late_a | late_b
    relay_from = jnp.where(early_a, 1, jnp.where(late_a, 3, jnp.where(late_b, 2, 0)))

    def remote(src, dst, send, recv, device):
        return pltpu.make_async_remote_copy(
            src_ref=src, dst_ref=dst, send_sem=send, recv_sem=recv, device_id=device, device_id_type=MESH
        )

    load = pltpu.make_async_copy(x_ref.at[0], own, own_sem)
    load.start()

    barrier = pltpu.get_barrier_semaphore()
    greeted = [above, below, sibling, partner, x_place(1), x_place(3)]
    greeted += [y_place(d) for d in range(1, 4)] + [z_place(d) for d in range(1, 8)]
    for device in greeted:
        pl.semaphore_signal(barrier, inc=1, device_id=device, device_id_type=MESH)

    def greet(device):
        pl.semaphore_signal(barrier, inc=1, device_id=device, device_id_type=MESH)

    @pl.when(meets)
    def _():
        greet(corner_place(low, 3, 7))
        greet(corner_place(low, 3, 1))
        greet(corner_place(low, 3, 2))

    @pl.when(hands_on)
    def _():
        greet(corner_place(1 - low, 3, 7))

    @pl.when(late_a | late_b)
    def _():
        greet(corner_place(low, 3, level + 3))

    more = jnp.where(leaves, 3, jnp.where(hands_on | late_a | late_b, 1, 0))
    pl.semaphore_wait(barrier, len(greeted) + more)

    def columns(j):
        return pl.ds(pl.multiple_of(j * CW, CW), CW)

    def ring_copy(j):
        return remote(x_ref.at[0, :, columns(j)], blocks.at[0, j], ys.at[j], yr.at[j], onward)

    def relay_copy(j):
        place = corner_place(
            jnp.where(j < 4, low, 1 - low), jnp.where(j < 4, 0, 3), jnp.where(j < 4, 0, 5 - lax.rem(j, 2))
        )
        slot = lax.rem(j // 2, 2)
        return remote(x_ref.at[0, :, columns(j)], relay.at[slot], ys.at[j], lw.at[slot], place)

    def handed_on(i):
        return remote(relay.at[i], relay.at[i], ls.at[i], lw.at[i], corner_place(low, 3, level - 3))

    def handed_in(i):
        j = 2 * i + jnp.where(meets, 1, jnp.where(late_a, 5, 4))
        place = corner_place(jnp.where(meets, 1 - low, low), 0, 0)
        return remote(relay.at[i], blocks.at[0, j], ls.at[i], yr.at[j], place)

    def own_copy(j):
        return remote(x_ref.at[0, :, columns(j)], blocks.at[1, j], ds.at[j], dr.at[j], sibling)

    def pass_copy(j):
        return remote(blocks.at[0, j], blocks.at[1, j], ds.at[j], dr.at[j], sibling)

    def pair_copy(j):
        return remote(sendb.at[j], recvb.at[j], xs.at[j], xr.at[j], partner)

    @pl.loop(0, NC)
    def _(j):
        i = j // 2
        chunk = jnp.where(leaves, jnp.where(lax.rem(j, 2) == 0, i + 1 - 2 * lax.rem(i, 2), 4 + i), j)
        by_relay = leaves & ((chunk >= 4) | (lax.rem(chunk, 2) == 1))

        @pl.when(by_relay)
        def _():
            relay_copy(chunk).start()

        @pl.when(jnp.logical_not(by_relay))
        def _():
            ring_copy(chunk).start()

        @pl.when(core == 0)
        def _():
            own_copy(j).start()

    for m in range(8):
        row = v_ref[0:1, m * 128:(m + 1) * 128]
        colv[m * 128:(m + 1) * 128, :] = jnp.broadcast_to(row, (128, 128)).T

    load.wait()

    @pl.loop(0, NAUX_HALF // 128)
    def _(i):
        rows = pl.ds(pl.multiple_of(i * 128, 128), 128)
        own_t[:, rows] = own[rows, :].T

    center = lax.rem(k - h - 2 * core * (1 - h) + NOCC, NOCC)
    other = lax.rem(center + 2 - h, NOCC)
    center_energy = eocc_ref[center]
    other_energy = eocc_ref[other]
    place = 1 - (1 - core) * (1 - h)

    def finish(j):
        pair_copy(j).wait_recv()
        vrow = v_ref[0:1, columns(j)]

        @pl.loop(0, 8)
        def _(m):
            rows = pl.ds(pl.multiple_of(m * 128, 128), 128)
            total = acc[j, rows, :] + recvb[j, rows, :].astype(f32)
            part = total / (colv[rows, :] + vrow - center_energy - other_energy)
            lr[place, rows, columns(j)] = part.astype(bf16)
            lr[1 - place, columns(j), rows] = part.T.astype(bf16)

    def product(stream, j):
        @pl.when(stream == 0)
        def _():
            ring_copy(j).wait_recv()

            @pl.when(up)
            def _():
                pass_copy(j).start()

            turn = j - relay_from
            slot = lax.rem(jnp.maximum(turn, 0) // 2, 2)

            @pl.when((hands_on | hands_in) & (turn >= 0) & (turn < 4) & (lax.rem(turn + 8, 2) == 0))
            def _():
                handed_on(slot).wait_recv()

                @pl.when(hands_on)
                def _():
                    handed_on(slot).start()

                @pl.when(hands_in)
                def _():
                    handed_in(slot).start()

        @pl.when(stream == 1)
        def _():
            own_copy(j).wait_recv()

        @pl.when(stream == h)
        def _():
            for m in range(4):
                rows = pl.ds(m * 256, 256)
                acc[j, rows, :] = jnp.dot(own_t[rows, :], blocks[stream, j], preferred_element_type=f32)

        @pl.when(stream != h)
        def _():
            for m in range(4):
                rows = pl.ds(m * 256, 256)
                sendb[j, rows, :] = jnp.dot(
                    own_t[rows, :], blocks[stream, j], preferred_element_type=f32
                ).astype(bf16)
            pair_copy(j).start()

    @pl.loop(0, NC + 1)
    def _(j):
        @pl.loop(0, 3)
        def _(q):
            early = up & (q < 2)
            stream = jnp.where(up, jnp.where(early, 1, 0), jnp.where(q == 0, 1 - h, h))
            chunk = jnp.where(early, 2 * j + q, j)

            @pl.when((j < NC) & jnp.where(up, (q == 2) | (j < NC // 2), q < 2))
            def _():
                product(stream, chunk)

        @pl.when(j > 0)
        def _():
            finish(j - 1)

    def tilde_rows(i, term):
        rows = pl.ds(pl.multiple_of(i * 128, 128), 128)
        left = lr[0, rows, :].astype(f32)
        right = lr[1, rows, :].astype(f32)
        tilde = (2.0 * right - left).astype(bf16)
        tt[rows, :] = tilde
        return term + jnp.sum((right * tilde.astype(f32)).reshape(16, 8, 8, 128), axis=(0, 2))

    term = lax.fori_loop(0, 8, tilde_rows, jnp.zeros((8, 128), f32))
    tbuf[h] = jnp.full((8, 128), -(2.0 / NVIR) * jnp.sum(term), f32)
    term_copy = remote(tbuf.at[h], tbuf.at[h], ts.at[0], tr.at[0], partner)
    term_copy.start()

    def core_copy(i):
        rows = pl.ds(i * 4, 4)
        return remote(dens.at[rows, :, 1 - core], dens_in.at[rows], cs.at[i], cr.at[i], sibling)

    @pl.loop(0, 4)
    def _(i):
        rows = pl.ds(pl.multiple_of(i * 256, 256), 256)
        out = 2.0 * jnp.dot(lr[0, rows, :], tt[...], preferred_element_type=f32)
        dens[pl.ds(i * 4, 4)] = out.reshape(4, 4, 2, 8, NVIR)
        core_copy(i).start()

    @pl.loop(0, 4)
    def _(i):
        core_copy(i).wait_recv()

    def x_term(to):
        rows = pl.ds(lax.rem(to, 2) * 8, 8)
        cols = pl.ds(pl.multiple_of((to // 2) * HALF, QUARTER), QUARTER)
        return dens[rows, :, core, :, cols] + dens_in[rows, :, :, cols]

    def y_term(to, side):
        cols = pl.ds(side * HALF + QUARTER, QUARTER)
        return dens[:, to, core, :, cols] + dens_in[:, to, :, cols]

    def first_copy(way, d):
        i = way * 3 + d - 1
        to = y_place(d) if way else x_place(d)
        return remote(first_out.at[way, d - 1], first_in.at[way, d - 1], fs.at[i], fr.at[i], to)

    for d in (2, 1, 3):
        first_out[0, d - 1] = x_term(lax.rem(x + d, 4)).reshape(256, QUARTER).astype(bf16)
        first_copy(0, d).start()
        for side in range(2):
            rows = pl.ds(side * 128, 128)
            first_out[1, d - 1, rows] = y_term(lax.rem(y + d, 4), side).reshape(128, QUARTER).astype(bf16)
        first_copy(1, d).start()
    xsum[...] = x_term(x)
    for side in range(2):
        ysum[side] = y_term(y, side)

    term_copy.wait()
    step_copy = remote(tbuf.at[0], tbuf.at[2], ts.at[1], tr.at[1], above)
    step_copy.start()

    for d in (1, 3, 2):
        first_copy(0, d).wait_recv()
        xsum[...] += first_in[0, d - 1].astype(f32).reshape(8, 4, 8, QUARTER)
        first_copy(1, d).wait_recv()
        ysum[...] += first_in[1, d - 1].astype(f32).reshape(2, 16, 8, QUARTER)

    def second_copy(way, d):
        i = way * 3 + d - 1
        to = x_place(d) if way else y_place(d)
        return remote(second_out.at[way, d - 1], second_in.at[way, d - 1], us.at[i], ur.at[i], to)

    def x_rest(to):
        return ysum[to // 2, pl.ds(lax.rem(to, 2) * 8, 8)]

    for d in (2, 1, 3):
        second_out[0, d - 1] = xsum[:, lax.rem(y + d, 4)].reshape(64, QUARTER).astype(bf16)
        second_copy(0, d).start()
        second_out[1, d - 1] = x_rest(lax.rem(x + d, 4)).reshape(64, QUARTER).astype(bf16)
        second_copy(1, d).start()
    left, right = xsum[:, y], x_rest(x)
    for d in (1, 3, 2):
        second_copy(0, d).wait_recv()
        left = left + second_in[0, d - 1].astype(f32).reshape(8, 8, QUARTER)
        second_copy(1, d).wait_recv()
        right = right + second_in[1, d - 1].astype(f32).reshape(8, 8, QUARTER)
    gsum[:, :, :QUARTER] = left
    gsum[:, :, QUARTER:] = right

    z_copies = []
    for d in (4, 3, 5, 2, 6, 1, 7):
        copy = remote(gsum.at[lax.rem(z + d, 8)], rz.at[d - 1], zs.at[d - 1], zr.at[d - 1], z_place(d))
        copy.start()
        z_copies.append(copy)

    step_copy.wait_recv()
    diag_ref[...] = tbuf[1] + jnp.where(core == 0, tbuf[2], tbuf[0])

    for copy in z_copies:
        copy.wait_recv()
    total = gsum[z]
    for d in range(7):
        total = total + rz[d]
    dens_ref[...] = total

    step_copy.wait_send()
    for copy in z_copies:
        copy.wait_send()
    for way in range(2):
        for d in range(1, 4):
            first_copy(way, d).wait_send()
            second_copy(way, d).wait_send()

    @pl.loop(0, 4)
    def _(i):
        core_copy(i).wait_send()

        @pl.when((i < 2) & (hands_on | hands_in))
        def _():
            handed_on(lax.rem(i, 2)).wait_send()

    @pl.loop(0, NC)
    def _(j):
        ring_copy(j).wait_send()
        own_copy(j).wait_send()
        pair_copy(j).wait_send()


def per_device(cholesky, occ_energy, vir_energy):
    dma = pltpu.SemaphoreType.DMA
    vmem = pltpu.VMEM
    dens, diag = pl.pallas_call(
        kernel,
        out_shape=(jax.ShapeDtypeStruct((8, HALF), f32), jax.ShapeDtypeStruct((8, 128), f32)),
        in_specs=[
            pl.BlockSpec(memory_space=pl.ANY),
            pl.BlockSpec(memory_space=pltpu.SMEM),
            pl.BlockSpec(memory_space=pltpu.VMEM),
        ],
        out_specs=(pl.BlockSpec(memory_space=pltpu.VMEM), pl.BlockSpec(memory_space=pltpu.VMEM)),
        scratch_shapes=[
            vmem((NAUX_HALF, NVIR), bf16),
            vmem((NVIR, NAUX_HALF), bf16),
            vmem((2, NC, NAUX_HALF, CW), bf16),
            vmem((2, NAUX_HALF, CW), bf16),
            vmem((NC, NVIR, CW), bf16),
            vmem((NC, NVIR, CW), bf16),
            vmem((NC, NVIR, CW), f32),
            vmem((2, NVIR, NVIR), bf16),
            vmem((NVIR, NVIR), bf16),
            vmem((16, 4, 2, 8, NVIR), f32),
            vmem((16, 4, 8, NVIR), f32),
            vmem((2, 3, 256, QUARTER), bf16),
            vmem((2, 3, 256, QUARTER), bf16),
            vmem((2, 3, 64, QUARTER), bf16),
            vmem((2, 3, 64, QUARTER), bf16),
            vmem((8, 4, 8, QUARTER), f32),
            vmem((2, 16, 8, QUARTER), f32),
            vmem((8, 8, HALF), f32),
            vmem((7, 8, HALF), f32),
            vmem((3, 8, 128), f32),
            vmem((NVIR, 128), f32),
            dma(()),
            dma((NC,)), dma((NC,)), dma((NC,)), dma((NC,)), dma((NC,)), dma((NC,)),
            dma((2,)), dma((2,)), dma((4,)), dma((4,)),
            dma((6,)), dma((6,)), dma((6,)), dma((6,)), dma((7,)), dma((7,)), dma((2,)), dma((2,)),
        ],
        compiler_params=pltpu.CompilerParams(
            collective_id=0, has_side_effects=True, vmem_limit_bytes=58 * 2**20
        ),
        cost_estimate=pl.CostEstimate(flops=13_000_000_000, bytes_accessed=16_000_000, transcendentals=0),
    )(cholesky, occ_energy, vir_energy.reshape(1, NVIR))
    return dens, diag[0, :1]


def solution(mesh):
    in_specs = (P("occ", "aux", None), P(), P())
    out_specs = (P("occ", "aux"), P("occ"))
    return jax.shard_map(
        per_device, mesh=mesh, in_specs=in_specs, out_specs=out_specs, check_vma=False
    )
```

```python
import functools

import jax
import jax.numpy as jnp
from jax import lax
from jax.experimental import pallas as pl
from jax.experimental.pallas import tpu as pltpu
from jax.sharding import PartitionSpec as P

MESH = pl.DeviceIdType.MESH
NAUX_HALF = 2560
NVIR = 1024
NOCC = 128
NC = 8
CW = NVIR // NC
LAG = 2
HALF = NVIR // 2
QUARTER = NVIR // 4
f32 = jnp.float32
bf16 = jnp.bfloat16


def kernel(
    x_ref, eocc_ref, v_ref, dens_ref, diag_ref,
    own, own_t, blocks, relay, sendb, recvb, acc, lr, tt, dens, dens_in,
    first_out, first_in, second_out, second_in, xsum, ysum, gsum, rz, tbuf, colv,
    own_sem, ys, yr, ds, dr, xs, xr, ls, lw, cs, cr, fs, fr, us, ur, zs, zr, ts, tr,
):
    k = lax.axis_index("occ")
    h = lax.axis_index("aux")
    core = lax.rem(k, 2)
    y = lax.rem(k // 2, 4)
    z = lax.rem(k // 8, 8)
    x = h * 2 + k // 64
    inner = lax.rem(k, 64)

    def x_place(d):
        to = lax.rem(x + d, 4)
        return {"occ": lax.rem(to, 2) * 64 + inner, "aux": to // 2}

    def y_place(d):
        return {"occ": k + (lax.rem(y + d, 4) - y) * 2, "aux": h}

    def z_place(d):
        return {"occ": k + (lax.rem(z + d, 8) - z) * 8, "aux": h}

    above = {"occ": lax.rem(k + 2, NOCC), "aux": h}
    below = {"occ": lax.rem(k + NOCC - 2, NOCC), "aux": h}
    sibling = {"occ": k + 1 - 2 * core, "aux": h}
    partner = {"occ": k, "aux": 1 - h}
    onward = {"occ": lax.rem(k + NOCC - 2 + 4 * core, NOCC), "aux": h}

    up = core == 1
    low = k // 64
    row, level = jnp.where(up, y, 3 - y), jnp.where(up, z, 7 - z)

    def corner_place(low, row, level):
        inner = jnp.where(up, level * 8 + row * 2, (7 - level) * 8 + (3 - row) * 2) + core
        return {"occ": low * 64 + inner, "aux": h}

    def at(row_is, level_is):
        return (row == row_is) & (level == level_is)

    leaves, meets = at(3, 7), at(0, 0)
    early_a, early_b, late_a, late_b = at(3, 4), at(3, 5), at(3, 1), at(3, 2)
    hands_on = early_a | early_b
    hands_in = meets | late_a | late_b
    relay_from = jnp.where(early_a, 1, jnp.where(late_a, 3, jnp.where(late_b, 2, 0)))
    relay_each = jnp.where(meets, 1, 2)

    def remote(src, dst, send, recv, device):
        return pltpu.make_async_remote_copy(
            src_ref=src, dst_ref=dst, send_sem=send, recv_sem=recv, device_id=device, device_id_type=MESH
        )

    load = pltpu.make_async_copy(x_ref.at[0], own, own_sem)
    load.start()

    barrier = pltpu.get_barrier_semaphore()
    greeted = [above, below, sibling, partner, x_place(1), x_place(3)]
    greeted += [y_place(d) for d in range(1, 4)] + [z_place(d) for d in range(1, 8)]
    for device in greeted:
        pl.semaphore_signal(barrier, inc=1, device_id=device, device_id_type=MESH)

    def greet(device):
        pl.semaphore_signal(barrier, inc=1, device_id=device, device_id_type=MESH)

    @pl.when(meets)
    def _():
        greet(corner_place(low, 3, 7))
        greet(corner_place(low, 3, 1))
        greet(corner_place(low, 3, 2))

    @pl.when(hands_on)
    def _():
        greet(corner_place(1 - low, 3, 7))

    @pl.when(late_a | late_b)
    def _():
        greet(corner_place(low, 3, level + 3))

    more = jnp.where(leaves, 3, jnp.where(hands_on | late_a | late_b, 1, 0))
    pl.semaphore_wait(barrier, len(greeted) + more)

    def columns(j):
        return pl.ds(pl.multiple_of(j * CW, CW), CW)

    def ring_copy(j):
        return remote(x_ref.at[0, :, columns(j)], blocks.at[0, j], ys.at[j], yr.at[j], onward)

    def relay_copy(j):
        place = corner_place(
            jnp.where(j < 4, low, 1 - low), jnp.where(j < 4, 0, 3), jnp.where(j < 4, 0, 5 - lax.rem(j, 2))
        )
        slot = jnp.where(j < 4, lax.rem(j, 2), lax.rem(j // 2, 2))
        return remote(x_ref.at[0, :, columns(j)], relay.at[slot], ys.at[j], lw.at[slot], place)

    def handed_on(i):
        return remote(relay.at[i], relay.at[i], ls.at[i], lw.at[i], corner_place(low, 3, level - 3))

    def handed_in(i):
        j = jnp.where(meets, i, 2 * i + jnp.where(late_a, 5, 4))
        place = corner_place(jnp.where(meets, 1 - low, low), 0, 0)
        return remote(relay.at[i], blocks.at[0, j], ls.at[i], yr.at[j], place)

    def own_copy(j):
        return remote(x_ref.at[0, :, columns(j)], blocks.at[1, j], ds.at[j], dr.at[j], sibling)

    def pass_copy(j):
        return remote(blocks.at[0, j], blocks.at[1, j], ds.at[j], dr.at[j], sibling)

    def pair_copy(j):
        return remote(sendb.at[j], recvb.at[j], xs.at[j], xr.at[j], partner)

    @pl.loop(0, NC)
    def _(j):
        by_relay = leaves & ((j >= 4) | (j < 2))

        @pl.when(by_relay)
        def _():
            relay_copy(j).start()

        @pl.when(jnp.logical_not(by_relay))
        def _():
            ring_copy(j).start()

        @pl.when(core == 0)
        def _():
            own_copy(j).start()

    for m in range(8):
        row = v_ref[0:1, m * 128:(m + 1) * 128]
        colv[m * 128:(m + 1) * 128, :] = jnp.broadcast_to(row, (128, 128)).T

    load.wait()

    @pl.loop(0, NAUX_HALF // 128)
    def _(i):
        rows = pl.ds(pl.multiple_of(i * 128, 128), 128)
        own_t[:, rows] = own[rows, :].T

    center = lax.rem(k - h - 2 * core * (1 - h) + NOCC, NOCC)
    other = lax.rem(center + 2 - h, NOCC)
    center_energy = eocc_ref[center]
    other_energy = eocc_ref[other]
    place = 1 - (1 - core) * (1 - h)

    def finish(j):
        pair_copy(j).wait_recv()
        vrow = v_ref[0:1, columns(j)]

        for m in range(8):
            rows = pl.ds(m * 128, 128)
            total = acc[j, rows, :] + recvb[j, rows, :].astype(f32)
            part = total / (colv[rows, :] + vrow - center_energy - other_energy)
            lr[place, rows, columns(j)] = part.astype(bf16)
            lr[1 - place, columns(j), rows] = part.T.astype(bf16)

    def product(stream, j):
        @pl.when(stream == 0)
        def _():
            ring_copy(j).wait_recv()

            @pl.when(up)
            def _():
                pass_copy(j).start()

        @pl.when(stream == 1)
        def _():
            own_copy(j).wait_recv()

        @pl.when(stream == h)
        def _():
            for m in range(4):
                rows = pl.ds(m * 256, 256)
                acc[j, rows, :] = jnp.dot(own_t[rows, :], blocks[stream, j], preferred_element_type=f32)

        @pl.when(stream != h)
        def _():
            for m in range(4):
                rows = pl.ds(m * 256, 256)
                sendb[j, rows, :] = jnp.dot(
                    own_t[rows, :], blocks[stream, j], preferred_element_type=f32
                ).astype(bf16)
            pair_copy(j).start()

    late_ring = meets
    late_passed = (core == 0) & (y == 0) & (z == 0)
    lag = jnp.where(late_ring | late_passed, LAG, 0)
    sooner = jnp.where(late_ring, 1, jnp.where(late_passed, 0, 1 - h))

    @pl.loop(0, NC + LAG + 1)
    def _(j):
        @pl.loop(0, 3)
        def _(q):
            early = up & (q < 2)
            stream = jnp.where(up, jnp.where(early, 1, 0), jnp.where(q == 0, sooner, 1 - sooner))
            turn = jnp.where(early, 2 * j + q, jnp.where(q == 0, j, j - lag))

            @pl.when((turn >= 0) & (turn < NC) & (up | (q < 2)))
            def _():
                product(stream, turn)

        since = j - relay_from
        slot = jnp.where(since == 0, 0, 1)

        @pl.when((hands_on | hands_in) & ((since == 0) | (since == relay_each)))
        def _():
            handed_on(slot).wait_recv()

            @pl.when(hands_on)
            def _():
                handed_on(slot).start()

            @pl.when(hands_in)
            def _():
                handed_in(slot).start()

        done = j - 1 - lag

        @pl.when((done >= 0) & (done < NC))
        def _():
            finish(done)

    def tilde_rows(i, term):
        rows = pl.ds(pl.multiple_of(i * 128, 128), 128)
        left = lr[0, rows, :].astype(f32)
        right = lr[1, rows, :].astype(f32)
        tilde = (2.0 * right - left).astype(bf16)
        tt[rows, :] = tilde
        return term + jnp.sum((right * tilde.astype(f32)).reshape(16, 8, 8, 128), axis=(0, 2))

    term = lax.fori_loop(0, 8, tilde_rows, jnp.zeros((8, 128), f32))
    tbuf[h] = jnp.full((8, 128), -(2.0 / NVIR) * jnp.sum(term), f32)
    term_copy = remote(tbuf.at[h], tbuf.at[h], ts.at[0], tr.at[0], partner)
    term_copy.start()

    def core_copy(i):
        rows = pl.ds(i * 4, 4)
        return remote(dens.at[rows, :, 1 - core], dens_in.at[rows], cs.at[i], cr.at[i], sibling)

    @pl.loop(0, 4)
    def _(i):
        rows = pl.ds(pl.multiple_of(i * 256, 256), 256)
        out = 2.0 * jnp.dot(lr[0, rows, :], tt[...], preferred_element_type=f32)
        dens[pl.ds(i * 4, 4)] = out.reshape(4, 4, 2, 8, NVIR)
        core_copy(i).start()

    @pl.loop(0, 4)
    def _(i):
        core_copy(i).wait_recv()

    def x_term(to):
        rows = pl.ds(lax.rem(to, 2) * 8, 8)
        cols = pl.ds(pl.multiple_of((to // 2) * HALF, QUARTER), QUARTER)
        return dens[rows, :, core, :, cols] + dens_in[rows, :, :, cols]

    def y_term(to, side):
        cols = pl.ds(side * HALF + QUARTER, QUARTER)
        return dens[:, to, core, :, cols] + dens_in[:, to, :, cols]

    def first_copy(way, d):
        i = way * 3 + d - 1
        to = y_place(d) if way else x_place(d)
        return remote(first_out.at[way, d - 1], first_in.at[way, d - 1], fs.at[i], fr.at[i], to)

    for d in (2, 1, 3):
        first_out[0, d - 1] = x_term(lax.rem(x + d, 4)).reshape(256, QUARTER).astype(bf16)
        first_copy(0, d).start()
        for side in range(2):
            rows = pl.ds(side * 128, 128)
            first_out[1, d - 1, rows] = y_term(lax.rem(y + d, 4), side).reshape(128, QUARTER).astype(bf16)
        first_copy(1, d).start()
    xsum[...] = x_term(x)
    for side in range(2):
        ysum[side] = y_term(y, side)

    term_copy.wait()
    step_copy = remote(tbuf.at[0], tbuf.at[2], ts.at[1], tr.at[1], above)
    step_copy.start()

    for d in (1, 3, 2):
        first_copy(0, d).wait_recv()
        xsum[...] += first_in[0, d - 1].astype(f32).reshape(8, 4, 8, QUARTER)
        first_copy(1, d).wait_recv()
        ysum[...] += first_in[1, d - 1].astype(f32).reshape(2, 16, 8, QUARTER)

    def second_copy(way, d):
        i = way * 3 + d - 1
        to = x_place(d) if way else y_place(d)
        return remote(second_out.at[way, d - 1], second_in.at[way, d - 1], us.at[i], ur.at[i], to)

    def x_rest(to):
        return ysum[to // 2, pl.ds(lax.rem(to, 2) * 8, 8)]

    for d in (2, 1, 3):
        second_out[0, d - 1] = xsum[:, lax.rem(y + d, 4)].reshape(64, QUARTER).astype(bf16)
        second_copy(0, d).start()
        second_out[1, d - 1] = x_rest(lax.rem(x + d, 4)).reshape(64, QUARTER).astype(bf16)
        second_copy(1, d).start()
    left, right = xsum[:, y], x_rest(x)
    for d in (1, 3, 2):
        second_copy(0, d).wait_recv()
        left = left + second_in[0, d - 1].astype(f32).reshape(8, 8, QUARTER)
        second_copy(1, d).wait_recv()
        right = right + second_in[1, d - 1].astype(f32).reshape(8, 8, QUARTER)
    gsum[:, :, :QUARTER] = left
    gsum[:, :, QUARTER:] = right

    z_copies = []
    for d in (4, 3, 5, 2, 6, 1, 7):
        copy = remote(gsum.at[lax.rem(z + d, 8)], rz.at[d - 1], zs.at[d - 1], zr.at[d - 1], z_place(d))
        copy.start()
        z_copies.append(copy)

    step_copy.wait_recv()
    diag_ref[...] = tbuf[1] + jnp.where(core == 0, tbuf[2], tbuf[0])

    for copy in z_copies:
        copy.wait_recv()
    total = gsum[z]
    for d in range(7):
        total = total + rz[d]
    dens_ref[...] = total

    step_copy.wait_send()
    for copy in z_copies:
        copy.wait_send()
    for way in range(2):
        for d in range(1, 4):
            first_copy(way, d).wait_send()
            second_copy(way, d).wait_send()

    @pl.loop(0, 4)
    def _(i):
        core_copy(i).wait_send()

        @pl.when((i < 2) & (hands_on | hands_in))
        def _():
            handed_on(lax.rem(i, 2)).wait_send()

    @pl.loop(0, NC)
    def _(j):
        ring_copy(j).wait_send()
        own_copy(j).wait_send()
        pair_copy(j).wait_send()


def per_device(cholesky, occ_energy, vir_energy):
    dma = pltpu.SemaphoreType.DMA
    vmem = pltpu.VMEM
    dens, diag = pl.pallas_call(
        kernel,
        out_shape=(jax.ShapeDtypeStruct((8, HALF), f32), jax.ShapeDtypeStruct((8, 128), f32)),
        in_specs=[
            pl.BlockSpec(memory_space=pl.ANY),
            pl.BlockSpec(memory_space=pltpu.SMEM),
            pl.BlockSpec(memory_space=pltpu.VMEM),
        ],
        out_specs=(pl.BlockSpec(memory_space=pltpu.VMEM), pl.BlockSpec(memory_space=pltpu.VMEM)),
        scratch_shapes=[
            vmem((NAUX_HALF, NVIR), bf16),
            vmem((NVIR, NAUX_HALF), bf16),
            vmem((2, NC, NAUX_HALF, CW), bf16),
            vmem((2, NAUX_HALF, CW), bf16),
            vmem((NC, NVIR, CW), bf16),
            vmem((NC, NVIR, CW), bf16),
            vmem((NC, NVIR, CW), f32),
            vmem((2, NVIR, NVIR), bf16),
            vmem((NVIR, NVIR), bf16),
            vmem((16, 4, 2, 8, NVIR), f32),
            vmem((16, 4, 8, NVIR), f32),
            vmem((2, 3, 256, QUARTER), bf16),
            vmem((2, 3, 256, QUARTER), bf16),
            vmem((2, 3, 64, QUARTER), bf16),
            vmem((2, 3, 64, QUARTER), bf16),
            vmem((8, 4, 8, QUARTER), f32),
            vmem((2, 16, 8, QUARTER), f32),
            vmem((8, 8, HALF), f32),
            vmem((7, 8, HALF), f32),
            vmem((3, 8, 128), f32),
            vmem((NVIR, 128), f32),
            dma(()),
            dma((NC,)), dma((NC,)), dma((NC,)), dma((NC,)), dma((NC,)), dma((NC,)),
            dma((2,)), dma((2,)), dma((4,)), dma((4,)),
            dma((6,)), dma((6,)), dma((6,)), dma((6,)), dma((7,)), dma((7,)), dma((2,)), dma((2,)),
        ],
        compiler_params=pltpu.CompilerParams(
            collective_id=0, has_side_effects=True, vmem_limit_bytes=58 * 2**20
        ),
        cost_estimate=pl.CostEstimate(flops=13_000_000_000, bytes_accessed=16_000_000, transcendentals=0),
    )(cholesky, occ_energy, vir_energy.reshape(1, NVIR))
    return dens, diag[0, :1]


def solution(mesh):
    in_specs = (P("occ", "aux", None), P(), P())
    out_specs = (P("occ", "aux"), P("occ"))
    return jax.shard_map(
        per_device, mesh=mesh, in_specs=in_specs, out_specs=out_specs, check_vma=False
    )
```

```python
import functools

import jax
import jax.numpy as jnp
from jax import lax
from jax.experimental import pallas as pl
from jax.experimental.pallas import tpu as pltpu
from jax.sharding import PartitionSpec as P

MESH = pl.DeviceIdType.MESH
NAUX_HALF = 2560
NVIR = 1024
NOCC = 128
NC = 8
CW = NVIR // NC
LAG = 2
PART = NAUX_HALF // 2
HALF = NVIR // 2
QUARTER = NVIR // 4
f32 = jnp.float32
bf16 = jnp.bfloat16


def kernel(
    x_ref, eocc_ref, v_ref, dens_ref, diag_ref,
    own, own_t, blocks, relay, sendb, recvb, acc, lr, tt, dens, dens_in,
    x_out, x_in, y_out, y_in, second_out, second_in, xsum, ysum, gsum, rz, tbuf, colv,
    own_sem, ys, yr, ds, dr, xs, xr, vs, ls, lw, cs, cr, fs, fr, gs, gr, us, ur, zs, zr, ts, tr,
):
    k = lax.axis_index("occ")
    h = lax.axis_index("aux")
    core = lax.rem(k, 2)
    y = lax.rem(k // 2, 4)
    z = lax.rem(k // 8, 8)
    x = h * 2 + k // 64
    inner = lax.rem(k, 64)

    def x_place(d):
        to = lax.rem(x + d, 4)
        return {"occ": lax.rem(to, 2) * 64 + inner, "aux": to // 2}

    def y_place(d):
        return {"occ": k + (lax.rem(y + d, 4) - y) * 2, "aux": h}

    def z_place(d):
        return {"occ": k + (lax.rem(z + d, 8) - z) * 8, "aux": h}

    above = {"occ": lax.rem(k + 2, NOCC), "aux": h}
    below = {"occ": lax.rem(k + NOCC - 2, NOCC), "aux": h}
    sibling = {"occ": k + 1 - 2 * core, "aux": h}
    partner = {"occ": k, "aux": 1 - h}
    onward = {"occ": lax.rem(k + NOCC - 2 + 4 * core, NOCC), "aux": h}

    up = core == 1
    low = k // 64
    row, level = jnp.where(up, y, 3 - y), jnp.where(up, z, 7 - z)

    def corner_place(low, row, level):
        inner = jnp.where(up, level * 8 + row * 2, (7 - level) * 8 + (3 - row) * 2) + core
        return {"occ": low * 64 + inner, "aux": h}

    def at(row_is, level_is):
        return (row == row_is) & (level == level_is)

    leaves, meets = at(3, 7), at(0, 0)
    early_a, early_b, late_a, late_b = at(3, 4), at(3, 5), at(3, 1), at(3, 2)
    hands_on = early_a | early_b
    hands_in = meets | late_a | late_b
    relay_from = jnp.where(early_a, 1, jnp.where(late_a, 2, jnp.where(late_b, 1, 0)))
    relay_each = jnp.where(meets, 1, 2)

    def remote(src, dst, send, recv, device):
        return pltpu.make_async_remote_copy(
            src_ref=src, dst_ref=dst, send_sem=send, recv_sem=recv, device_id=device, device_id_type=MESH
        )

    load = pltpu.make_async_copy(x_ref.at[0], own, own_sem)
    load.start()

    barrier = pltpu.get_barrier_semaphore()
    greeted = [above, below, sibling, partner, x_place(1), x_place(3)]
    greeted += [y_place(d) for d in range(1, 4)] + [z_place(d) for d in range(1, 8)]
    for device in greeted:
        pl.semaphore_signal(barrier, inc=1, device_id=device, device_id_type=MESH)

    def greet(device):
        pl.semaphore_signal(barrier, inc=1, device_id=device, device_id_type=MESH)

    @pl.when(meets)
    def _():
        greet(corner_place(low, 3, 7))
        greet(corner_place(low, 3, 1))
        greet(corner_place(low, 3, 2))

    @pl.when(hands_on)
    def _():
        greet(corner_place(1 - low, 3, 7))

    @pl.when(late_a | late_b)
    def _():
        greet(corner_place(low, 3, level + 3))

    more = jnp.where(leaves, 3, jnp.where(hands_on | late_a | late_b, 1, 0))
    pl.semaphore_wait(barrier, len(greeted) + more)

    def columns(j):
        return pl.ds(pl.multiple_of(j * CW, CW), CW)

    def ring_copy(j):
        return remote(x_ref.at[0, :, columns(j)], blocks.at[0, j], ys.at[j], yr.at[j], onward)

    def relay_copy(j, part):
        place = corner_place(
            jnp.where(j < 4, low, 1 - low), jnp.where(j < 4, 0, 3), jnp.where(j < 4, 0, 5 - lax.rem(j, 2))
        )
        slot = jnp.where(j < 4, lax.rem(j, 2), lax.rem(j // 2, 2))
        rows = pl.ds(part * PART, PART)
        return remote(
            x_ref.at[0, rows, columns(j)], relay.at[slot, rows], vs.at[2 * j + part], lw.at[2 * slot + part], place
        )

    def handed_on(i, part):
        here = relay.at[i, pl.ds(part * PART, PART)]
        return remote(here, here, ls.at[2 * i + part], lw.at[2 * i + part], corner_place(low, 3, level - 3))

    def handed_in(i, part):
        j = jnp.where(meets, i, 2 * i + jnp.where(late_a, 5, 4))
        place = corner_place(jnp.where(meets, 1 - low, low), 0, 0)
        rows = pl.ds(part * PART, PART)
        return remote(relay.at[i, rows], blocks.at[0, j, rows], ls.at[2 * i + part], yr.at[j], place)

    def by_relay(j):
        return leaves & ((j >= 4) | (j < 2))

    def own_copy(j):
        return remote(x_ref.at[0, :, columns(j)], blocks.at[1, j], ds.at[j], dr.at[j], sibling)

    def pass_copy(j):
        return remote(blocks.at[0, j], blocks.at[1, j], ds.at[j], dr.at[j], sibling)

    def pair_copy(j):
        return remote(sendb.at[j], recvb.at[j], xs.at[j], xr.at[j], partner)

    @pl.loop(0, NC)
    def _(j):
        @pl.when(by_relay(j))
        def _():
            for part in range(2):
                relay_copy(j, part).start()

        @pl.when(jnp.logical_not(by_relay(j)))
        def _():
            ring_copy(j).start()

        @pl.when(core == 0)
        def _():
            own_copy(j).start()

    for m in range(8):
        row = v_ref[0:1, m * 128:(m + 1) * 128]
        colv[m * 128:(m + 1) * 128, :] = jnp.broadcast_to(row, (128, 128)).T

    load.wait()

    @pl.loop(0, NAUX_HALF // 128)
    def _(i):
        rows = pl.ds(pl.multiple_of(i * 128, 128), 128)
        own_t[:, rows] = own[rows, :].T

    center = lax.rem(k - h - 2 * core * (1 - h) + NOCC, NOCC)
    other = lax.rem(center + 2 - h, NOCC)
    center_energy = eocc_ref[center]
    other_energy = eocc_ref[other]
    place = 1 - (1 - core) * (1 - h)

    def finish(j):
        pair_copy(j).wait_recv()
        vrow = v_ref[0:1, columns(j)]

        for m in range(8):
            rows = pl.ds(m * 128, 128)
            total = acc[j, rows, :] + recvb[j, rows, :].astype(f32)
            part = total / (colv[rows, :] + vrow - center_energy - other_energy)
            lr[place, rows, columns(j)] = part.astype(bf16)
            lr[1 - place, columns(j), rows] = part.T.astype(bf16)

        strip = columns(j)
        tt[strip, :] = (2.0 * lr[1, strip, :].astype(f32) - lr[0, strip, :].astype(f32)).astype(bf16)
        tt[:, strip] = (2.0 * lr[1, :, strip].astype(f32) - lr[0, :, strip].astype(f32)).astype(bf16)

    def product(stream, j):
        @pl.when(stream == 0)
        def _():
            ring_copy(j).wait_recv()

            @pl.when(up)
            def _():
                pass_copy(j).start()

        @pl.when(stream == 1)
        def _():
            own_copy(j).wait_recv()

        @pl.when(stream == h)
        def _():
            for m in range(4):
                rows = pl.ds(m * 256, 256)
                acc[j, rows, :] = jnp.dot(own_t[rows, :], blocks[stream, j], preferred_element_type=f32)

        @pl.when(stream != h)
        def _():
            for m in range(4):
                rows = pl.ds(m * 256, 256)
                sendb[j, rows, :] = jnp.dot(
                    own_t[rows, :], blocks[stream, j], preferred_element_type=f32
                ).astype(bf16)
            pair_copy(j).start()

    late_ring = meets
    late_passed = (core == 0) & (y == 0) & (z == 0)
    lag = jnp.where(late_ring | late_passed, LAG, 0)
    sooner = jnp.where(late_ring, 1, jnp.where(late_passed, 0, 1 - h))

    @pl.loop(0, NC + LAG + 1)
    def _(j):
        @pl.loop(0, 3)
        def _(q):
            early = up & (q < 2)
            stream = jnp.where(up, jnp.where(early, 1, 0), jnp.where(q == 0, sooner, 1 - sooner))
            turn = jnp.where(early, 2 * j + q, jnp.where(q == 0, j, j - lag))

            @pl.when((turn >= 0) & (turn < NC) & (up | (q < 2)))
            def _():
                product(stream, turn)

        since = j - relay_from
        slot = jnp.where(since == 0, 0, 1)

        @pl.when((hands_on | hands_in) & ((since == 0) | (since == relay_each)))
        def _():
            for part in range(2):
                handed_on(slot, part).wait_recv()

                @pl.when(hands_on)
                def _():
                    handed_on(slot, part).start()

                @pl.when(hands_in)
                def _():
                    handed_in(slot, part).start()

        done = j - 1 - lag

        @pl.when((done >= 0) & (done < NC))
        def _():
            finish(done)

    def term_rows(i, term):
        rows = pl.ds(pl.multiple_of(i * 128, 128), 128)
        product = lr[1, rows, :].astype(f32) * tt[rows, :].astype(f32)
        return term + jnp.sum(product.reshape(16, 8, 8, 128), axis=(0, 2))

    def quadrant(q):
        d = jnp.where(q == 0, 2, jnp.where(q == 1, 1, jnp.where(q == 2, 3, 0)))
        to = lax.rem(x + d, 4)
        return d, to, lax.rem(to, 2), to // 2

    def core_copy(q):
        _, _, upper, side = quadrant(q)
        rows = pl.ds(upper * 8, 8)
        cols = pl.ds(pl.multiple_of(side * HALF, HALF), HALF)
        return remote(
            dens.at[rows, :, 1 - core, :, cols], dens_in.at[rows, :, :, cols], cs.at[q], cr.at[q], sibling
        )

    def x_copy(d):
        return remote(x_out.at[d - 1], x_in.at[d - 1], fs.at[d - 1], fr.at[d - 1], x_place(d))

    def y_copy(to, e):
        return remote(y_out.at[e - 1, to], y_in.at[e - 1, to], gs.at[e - 1, to], gr.at[e - 1], y_place(e))

    @pl.loop(0, 5)
    def _(q):
        @pl.when(q < 4)
        def _():
            _, _, upper, side = quadrant(q)
            rows = pl.ds(pl.multiple_of(upper * HALF, HALF), HALF)
            cols = pl.ds(pl.multiple_of(side * HALF, HALF), HALF)
            out = 2.0 * jnp.dot(lr[0, rows, :], tt[:, cols], preferred_element_type=f32)
            dens[pl.ds(upper * 8, 8), :, :, :, cols] = out.reshape(8, 4, 2, 8, HALF)
            core_copy(q).start()

        @pl.when(q > 0)
        def _():
            core_copy(q - 1).wait_recv()
            d, to, upper, side = quadrant(q - 1)
            rows = pl.ds(upper * 8, 8)
            left = pl.ds(pl.multiple_of(side * HALF, QUARTER), QUARTER)
            right = pl.ds(pl.multiple_of(side * HALF + QUARTER, QUARTER), QUARTER)
            part = dens[rows, :, core, :, left] + dens_in[rows, :, :, left]

            @pl.when(d == 0)
            def _():
                xsum[...] = part

            @pl.when(d > 0)
            def _():
                away = jnp.maximum(d, 1)
                x_out[away - 1] = part.reshape(256, QUARTER).astype(bf16)
                x_copy(away).start()

            for e in (2, 1, 3, 0):
                row = lax.rem(y + e, 4)
                part = dens[rows, row, core, :, right] + dens_in[rows, row, :, right]
                if e == 0:
                    ysum[to] = part
                else:
                    y_out[e - 1, to] = part.reshape(64, QUARTER).astype(bf16)
                    y_copy(to, e).start()

    term = lax.fori_loop(0, 8, term_rows, jnp.zeros((8, 128), f32))
    tbuf[h] = jnp.full((8, 128), -(2.0 / NVIR) * jnp.sum(term), f32)
    term_copy = remote(tbuf.at[h], tbuf.at[h], ts.at[0], tr.at[0], partner)
    term_copy.start()

    for d in (1, 3, 2):
        x_copy(d).wait_recv()
        xsum[...] += x_in[d - 1].astype(f32).reshape(8, 4, 8, QUARTER)
        remote(y_out.at[d - 1], y_in.at[d - 1], gs.at[d - 1, 0], gr.at[d - 1], y_place(d)).wait_recv()
        ysum[...] += y_in[d - 1].astype(f32).reshape(4, 8, 8, QUARTER)

    def second_copy(way, d):
        i = way * 3 + d - 1
        to = x_place(d) if way else y_place(d)
        return remote(second_out.at[way, d - 1], second_in.at[way, d - 1], us.at[i], ur.at[i], to)

    for d in (2, 1, 3):
        second_out[0, d - 1] = xsum[:, lax.rem(y + d, 4)].reshape(64, QUARTER).astype(bf16)
        second_copy(0, d).start()
        second_out[1, d - 1] = ysum[lax.rem(x + d, 4)].reshape(64, QUARTER).astype(bf16)
        second_copy(1, d).start()
    term_copy.wait()
    step_copy = remote(tbuf.at[0], tbuf.at[2], ts.at[1], tr.at[1], above)
    step_copy.start()

    left, right = xsum[:, y], ysum[x]
    for d in (1, 3, 2):
        second_copy(0, d).wait_recv()
        left = left + second_in[0, d - 1].astype(f32).reshape(8, 8, QUARTER)
        second_copy(1, d).wait_recv()
        right = right + second_in[1, d - 1].astype(f32).reshape(8, 8, QUARTER)
    gsum[:, :, :QUARTER] = left
    gsum[:, :, QUARTER:] = right

    z_copies = []
    for d in (4, 3, 5, 2, 6, 1, 7):
        copy = remote(gsum.at[lax.rem(z + d, 8)], rz.at[d - 1], zs.at[d - 1], zr.at[d - 1], z_place(d))
        copy.start()
        z_copies.append(copy)

    step_copy.wait_recv()
    diag_ref[...] = tbuf[1] + jnp.where(core == 0, tbuf[2], tbuf[0])

    for copy in z_copies:
        copy.wait_recv()
    total = gsum[z]
    for d in range(7):
        total = total + rz[d]
    dens_ref[...] = total

    step_copy.wait_send()
    for copy in z_copies:
        copy.wait_send()
    for way in range(2):
        for d in range(1, 4):
            second_copy(way, d).wait_send()
    for d in range(1, 4):
        x_copy(d).wait_send()

    @pl.loop(0, 4)
    def _(i):
        core_copy(i).wait_send()
        for e in range(1, 4):
            y_copy(i, e).wait_send()

        @pl.when((i < 2) & (hands_on | hands_in))
        def _():
            for part in range(2):
                handed_on(lax.rem(i, 2), part).wait_send()

    @pl.loop(0, NC)
    def _(j):
        @pl.when(by_relay(j))
        def _():
            for part in range(2):
                relay_copy(j, part).wait_send()

        @pl.when(jnp.logical_not(by_relay(j)))
        def _():
            ring_copy(j).wait_send()

        own_copy(j).wait_send()
        pair_copy(j).wait_send()


def per_device(cholesky, occ_energy, vir_energy):
    dma = pltpu.SemaphoreType.DMA
    vmem = pltpu.VMEM
    dens, diag = pl.pallas_call(
        kernel,
        out_shape=(jax.ShapeDtypeStruct((8, HALF), f32), jax.ShapeDtypeStruct((8, 128), f32)),
        in_specs=[
            pl.BlockSpec(memory_space=pl.ANY),
            pl.BlockSpec(memory_space=pltpu.SMEM),
            pl.BlockSpec(memory_space=pltpu.VMEM),
        ],
        out_specs=(pl.BlockSpec(memory_space=pltpu.VMEM), pl.BlockSpec(memory_space=pltpu.VMEM)),
        scratch_shapes=[
            vmem((NAUX_HALF, NVIR), bf16),
            vmem((NVIR, NAUX_HALF), bf16),
            vmem((2, NC, NAUX_HALF, CW), bf16),
            vmem((2, NAUX_HALF, CW), bf16),
            vmem((NC, NVIR, CW), bf16),
            vmem((NC, NVIR, CW), bf16),
            vmem((NC, NVIR, CW), f32),
            vmem((2, NVIR, NVIR), bf16),
            vmem((NVIR, NVIR), bf16),
            vmem((16, 4, 2, 8, NVIR), f32),
            vmem((16, 4, 8, NVIR), f32),
            vmem((3, 256, QUARTER), bf16),
            vmem((3, 256, QUARTER), bf16),
            vmem((3, 4, 64, QUARTER), bf16),
            vmem((3, 4, 64, QUARTER), bf16),
            vmem((2, 3, 64, QUARTER), bf16),
            vmem((2, 3, 64, QUARTER), bf16),
            vmem((8, 4, 8, QUARTER), f32),
            vmem((4, 8, 8, QUARTER), f32),
            vmem((8, 8, HALF), f32),
            vmem((7, 8, HALF), f32),
            vmem((3, 8, 128), f32),
            vmem((NVIR, 128), f32),
            dma(()),
            dma((NC,)), dma((NC,)), dma((NC,)), dma((NC,)), dma((NC,)), dma((NC,)),
            dma((2 * NC,)), dma((4,)), dma((4,)), dma((4,)), dma((4,)),
            dma((3,)), dma((3,)), dma((3, 4)), dma((3,)), dma((6,)), dma((6,)), dma((7,)), dma((7,)), dma((2,)), dma((2,)),
        ],
        compiler_params=pltpu.CompilerParams(
            collective_id=0, has_side_effects=True, vmem_limit_bytes=58 * 2**20
        ),
        cost_estimate=pl.CostEstimate(flops=13_000_000_000, bytes_accessed=16_000_000, transcendentals=0),
    )(cholesky, occ_energy, vir_energy.reshape(1, NVIR))
    return dens, diag[0, :1]


def solution(mesh):
    in_specs = (P("occ", "aux", None), P(), P())
    out_specs = (P("occ", "aux"), P("occ"))
    return jax.shard_map(
        per_device, mesh=mesh, in_specs=in_specs, out_specs=out_specs, check_vma=False
    )
```

```python
import functools

import jax
import jax.numpy as jnp
from jax import lax
from jax.experimental import pallas as pl
from jax.experimental.pallas import tpu as pltpu
from jax.sharding import PartitionSpec as P

MESH = pl.DeviceIdType.MESH
NAUX_HALF = 2560
NVIR = 1024
NOCC = 128
NC = 8
CW = NVIR // NC
LAG = 2
PART = NAUX_HALF // 2
HALF = NVIR // 2
QUARTER = NVIR // 4
f32 = jnp.float32
bf16 = jnp.bfloat16


def kernel(
    x_ref, eocc_ref, v_ref, dens_ref, diag_ref,
    own, own_t, blocks, relay, sendb, recvb, acc, lr, tt, dens, dens_in,
    x_out, x_in, y_out, y_in, second_out, second_in, xsum, ysum, gsum, rz, tbuf, colv,
    own_sem, ys, yr, ds, dr, xs, xr, vs, ls, lw, cs, cr, fs, fr, gs, gr, us, ur, zs, zr, ts, tr,
):
    k = lax.axis_index("occ")
    h = lax.axis_index("aux")
    core = lax.rem(k, 2)
    y = lax.rem(k // 2, 4)
    z = lax.rem(k // 8, 8)
    x = h * 2 + k // 64
    inner = lax.rem(k, 64)

    def x_place(d):
        to = lax.rem(x + d, 4)
        return {"occ": lax.rem(to, 2) * 64 + inner, "aux": to // 2}

    def y_place(d):
        return {"occ": k + (lax.rem(y + d, 4) - y) * 2, "aux": h}

    def z_place(d):
        return {"occ": k + (lax.rem(z + d, 8) - z) * 8, "aux": h}

    above = {"occ": lax.rem(k + 2, NOCC), "aux": h}
    below = {"occ": lax.rem(k + NOCC - 2, NOCC), "aux": h}
    sibling = {"occ": k + 1 - 2 * core, "aux": h}
    partner = {"occ": k, "aux": 1 - h}
    onward = {"occ": lax.rem(k + NOCC - 2 + 4 * core, NOCC), "aux": h}

    up = core == 1
    low = k // 64
    row, level = jnp.where(up, y, 3 - y), jnp.where(up, z, 7 - z)

    def corner_place(low, row, level):
        inner = jnp.where(up, level * 8 + row * 2, (7 - level) * 8 + (3 - row) * 2) + core
        return {"occ": low * 64 + inner, "aux": h}

    def at(row_is, level_is):
        return (row == row_is) & (level == level_is)

    leaves, meets = at(3, 7), at(0, 0)
    early_a, early_b, late_a, late_b = at(3, 4), at(3, 5), at(3, 1), at(3, 2)
    hands_on = early_a | early_b
    hands_in = meets | late_a | late_b
    relay_from = jnp.where(early_a, 1, jnp.where(late_a, 2, jnp.where(late_b, 1, 0)))
    relay_each = jnp.where(meets, 1, 2)

    def remote(src, dst, send, recv, device):
        return pltpu.make_async_remote_copy(
            src_ref=src, dst_ref=dst, send_sem=send, recv_sem=recv, device_id=device, device_id_type=MESH
        )

    load = pltpu.make_async_copy(x_ref.at[0], own, own_sem)
    load.start()

    barrier = pltpu.get_barrier_semaphore()
    greeted = [z_place(d) for d in (4, 3, 5, 2, 6, 1, 7)] + [y_place(d) for d in (2, 1, 3)]
    greeted += [partner, x_place(1), x_place(3), above, below, sibling]
    for device in greeted:
        pl.semaphore_signal(barrier, inc=1, device_id=device, device_id_type=MESH)

    def greet(device):
        pl.semaphore_signal(barrier, inc=1, device_id=device, device_id_type=MESH)

    @pl.when(meets)
    def _():
        greet(corner_place(low, 3, 7))
        greet(corner_place(low, 3, 1))
        greet(corner_place(low, 3, 2))

    @pl.when(hands_on)
    def _():
        greet(corner_place(1 - low, 3, 7))

    @pl.when(late_a | late_b)
    def _():
        greet(corner_place(low, 3, level + 3))

    more = jnp.where(leaves, 3, jnp.where(hands_on | late_a | late_b, 1, 0))
    pl.semaphore_wait(barrier, len(greeted) + more)

    def columns(j):
        return pl.ds(pl.multiple_of(j * CW, CW), CW)

    def ring_copy(j):
        return remote(x_ref.at[0, :, columns(j)], blocks.at[0, j], ys.at[j], yr.at[j], onward)

    def relay_copy(j, part):
        place = corner_place(
            jnp.where(j < 4, low, 1 - low), jnp.where(j < 4, 0, 3), jnp.where(j < 4, 0, 5 - lax.rem(j, 2))
        )
        slot = jnp.where(j < 4, lax.rem(j, 2), lax.rem(j // 2, 2))
        rows = pl.ds(part * PART, PART)
        return remote(
            x_ref.at[0, rows, columns(j)], relay.at[slot, rows], vs.at[2 * j + part], lw.at[2 * slot + part], place
        )

    def handed_on(i, part):
        here = relay.at[i, pl.ds(part * PART, PART)]
        return remote(here, here, ls.at[2 * i + part], lw.at[2 * i + part], corner_place(low, 3, level - 3))

    def handed_in(i, part):
        j = jnp.where(meets, i, 2 * i + jnp.where(late_a, 5, 4))
        place = corner_place(jnp.where(meets, 1 - low, low), 0, 0)
        rows = pl.ds(part * PART, PART)
        return remote(relay.at[i, rows], blocks.at[0, j, rows], ls.at[2 * i + part], yr.at[j], place)

    def by_relay(j):
        return leaves & ((j >= 4) | (j < 2))

    def own_copy(j):
        return remote(x_ref.at[0, :, columns(j)], blocks.at[1, j], ds.at[j], dr.at[j], sibling)

    def pass_copy(j):
        return remote(blocks.at[0, j], blocks.at[1, j], ds.at[j], dr.at[j], sibling)

    def pair_copy(j):
        return remote(sendb.at[j], recvb.at[j], xs.at[j], xr.at[j], partner)

    @pl.loop(0, NC)
    def _(j):
        @pl.when(by_relay(j))
        def _():
            for part in range(2):
                relay_copy(j, part).start()

        @pl.when(jnp.logical_not(by_relay(j)))
        def _():
            ring_copy(j).start()

        @pl.when(core == 0)
        def _():
            own_copy(j).start()

    for m in range(8):
        row = v_ref[0:1, m * 128:(m + 1) * 128]
        colv[m * 128:(m + 1) * 128, :] = jnp.broadcast_to(row, (128, 128)).T

    load.wait()

    @pl.loop(0, NAUX_HALF // 128)
    def _(i):
        rows = pl.ds(pl.multiple_of(i * 128, 128), 128)
        own_t[:, rows] = own[rows, :].T

    center = lax.rem(k - h - 2 * core * (1 - h) + NOCC, NOCC)
    other = lax.rem(center + 2 - h, NOCC)
    center_energy = eocc_ref[center]
    other_energy = eocc_ref[other]
    place = 1 - (1 - core) * (1 - h)

    def finish(j):
        pair_copy(j).wait_recv()
        vrow = v_ref[0:1, columns(j)]

        for m in range(8):
            rows = pl.ds(m * 128, 128)
            total = acc[j, rows, :] + recvb[j, rows, :].astype(f32)
            part = total / (colv[rows, :] + vrow - center_energy - other_energy)
            lr[place, rows, columns(j)] = part.astype(bf16)
            lr[1 - place, columns(j), rows] = part.T.astype(bf16)

        strip = columns(j)
        tt[strip, :] = (2.0 * lr[1, strip, :].astype(f32) - lr[0, strip, :].astype(f32)).astype(bf16)
        tt[:, strip] = (2.0 * lr[1, :, strip].astype(f32) - lr[0, :, strip].astype(f32)).astype(bf16)

    def product(stream, j):
        @pl.when(stream == 0)
        def _():
            ring_copy(j).wait_recv()

            @pl.when(up)
            def _():
                pass_copy(j).start()

        @pl.when(stream == 1)
        def _():
            own_copy(j).wait_recv()

        @pl.when(stream == h)
        def _():
            for m in range(4):
                rows = pl.ds(m * 256, 256)
                acc[j, rows, :] = jnp.dot(own_t[rows, :], blocks[stream, j], preferred_element_type=f32)

        @pl.when(stream != h)
        def _():
            for m in range(4):
                rows = pl.ds(m * 256, 256)
                sendb[j, rows, :] = jnp.dot(
                    own_t[rows, :], blocks[stream, j], preferred_element_type=f32
                ).astype(bf16)
            pair_copy(j).start()

    late_ring = meets
    late_passed = (core == 0) & (y == 0) & (z == 0)
    lag = jnp.where(late_ring | late_passed, LAG, 0)
    sooner = jnp.where(late_ring, 1, jnp.where(late_passed, 0, 1 - h))

    @pl.loop(0, NC + LAG + 1)
    def _(j):
        @pl.loop(0, 3)
        def _(q):
            early = up & (q < 2)
            stream = jnp.where(up, jnp.where(early, 1, 0), jnp.where(q == 0, sooner, 1 - sooner))
            turn = jnp.where(early, 2 * j + q, jnp.where(q == 0, j, j - lag))

            @pl.when((turn >= 0) & (turn < NC) & (up | (q < 2)))
            def _():
                product(stream, turn)

        since = j - relay_from
        slot = jnp.where(since == 0, 0, 1)

        @pl.when((hands_on | hands_in) & ((since == 0) | (since == relay_each)))
        def _():
            for part in range(2):
                handed_on(slot, part).wait_recv()

                @pl.when(hands_on)
                def _():
                    handed_on(slot, part).start()

                @pl.when(hands_in)
                def _():
                    handed_in(slot, part).start()

        done = j - 1 - lag

        @pl.when((done >= 0) & (done < NC))
        def _():
            finish(done)

    def term_rows(i, term):
        rows = pl.ds(pl.multiple_of(i * 128, 128), 128)
        product = lr[1, rows, :].astype(f32) * tt[rows, :].astype(f32)
        return term + jnp.sum(product.reshape(16, 8, 8, 128), axis=(0, 2))

    def quadrant(q):
        d = jnp.where(q == 0, 2, jnp.where(q == 1, 1, jnp.where(q == 2, 3, 0)))
        to = lax.rem(x + d, 4)
        return d, to, lax.rem(to, 2), to // 2

    def core_copy(q):
        _, _, upper, side = quadrant(q)
        rows = pl.ds(upper * 8, 8)
        cols = pl.ds(pl.multiple_of(side * HALF, HALF), HALF)
        return remote(
            dens.at[rows, :, 1 - core, :, cols], dens_in.at[rows, :, :, cols], cs.at[q], cr.at[q], sibling
        )

    def x_copy(d):
        return remote(x_out.at[d - 1], x_in.at[d - 1], fs.at[d - 1], fr.at[d - 1], x_place(d))

    def y_copy(to, e):
        return remote(y_out.at[e - 1, to], y_in.at[e - 1, to], gs.at[e - 1, to], gr.at[e - 1], y_place(e))

    @pl.loop(0, 5)
    def _(q):
        @pl.when(q < 4)
        def _():
            _, _, upper, side = quadrant(q)
            rows = pl.ds(pl.multiple_of(upper * HALF, HALF), HALF)
            cols = pl.ds(pl.multiple_of(side * HALF, HALF), HALF)
            out = 2.0 * jnp.dot(lr[0, rows, :], tt[:, cols], preferred_element_type=f32)
            dens[pl.ds(upper * 8, 8), :, :, :, cols] = out.reshape(8, 4, 2, 8, HALF)
            core_copy(q).start()

        @pl.when(q > 0)
        def _():
            core_copy(q - 1).wait_recv()
            d, to, upper, side = quadrant(q - 1)
            rows = pl.ds(upper * 8, 8)
            left = pl.ds(pl.multiple_of(side * HALF, QUARTER), QUARTER)
            right = pl.ds(pl.multiple_of(side * HALF + QUARTER, QUARTER), QUARTER)
            part = dens[rows, :, core, :, left] + dens_in[rows, :, :, left]

            @pl.when(d == 0)
            def _():
                xsum[...] = part

            @pl.when(d > 0)
            def _():
                away = jnp.maximum(d, 1)
                x_out[away - 1] = part.reshape(256, QUARTER).astype(bf16)
                x_copy(away).start()

            for e in (2, 1, 3, 0):
                row = lax.rem(y + e, 4)
                part = dens[rows, row, core, :, right] + dens_in[rows, row, :, right]
                if e == 0:
                    ysum[to] = part
                else:
                    y_out[e - 1, to] = part.reshape(64, QUARTER).astype(bf16)
                    y_copy(to, e).start()

    term = lax.fori_loop(0, 8, term_rows, jnp.zeros((8, 128), f32))
    tbuf[h] = jnp.full((8, 128), -(2.0 / NVIR) * jnp.sum(term), f32)
    term_copy = remote(tbuf.at[h], tbuf.at[h], ts.at[0], tr.at[0], partner)
    term_copy.start()

    for d in (1, 3, 2):
        x_copy(d).wait_recv()
        xsum[...] += x_in[d - 1].astype(f32).reshape(8, 4, 8, QUARTER)
        remote(y_out.at[d - 1], y_in.at[d - 1], gs.at[d - 1, 0], gr.at[d - 1], y_place(d)).wait_recv()
        ysum[...] += y_in[d - 1].astype(f32).reshape(4, 8, 8, QUARTER)

    def second_copy(way, d):
        i = way * 3 + d - 1
        to = x_place(d) if way else y_place(d)
        return remote(second_out.at[way, d - 1], second_in.at[way, d - 1], us.at[i], ur.at[i], to)

    for d in (2, 1, 3):
        second_out[0, d - 1] = xsum[:, lax.rem(y + d, 4)].reshape(64, QUARTER).astype(bf16)
        second_copy(0, d).start()
        second_out[1, d - 1] = ysum[lax.rem(x + d, 4)].reshape(64, QUARTER).astype(bf16)
        second_copy(1, d).start()
    term_copy.wait()
    step_copy = remote(tbuf.at[0], tbuf.at[2], ts.at[1], tr.at[1], above)
    step_copy.start()

    left, right = xsum[:, y], ysum[x]
    for d in (1, 3, 2):
        second_copy(0, d).wait_recv()
        left = left + second_in[0, d - 1].astype(f32).reshape(8, 8, QUARTER)
        second_copy(1, d).wait_recv()
        right = right + second_in[1, d - 1].astype(f32).reshape(8, 8, QUARTER)
    gsum[:, :, :QUARTER] = left
    gsum[:, :, QUARTER:] = right

    z_copies = []
    for d in (4, 3, 5, 2, 6, 1, 7):
        copy = remote(gsum.at[lax.rem(z + d, 8)], rz.at[d - 1], zs.at[d - 1], zr.at[d - 1], z_place(d))
        copy.start()
        z_copies.append(copy)

    for way in range(2):
        for d in range(1, 4):
            second_copy(way, d).wait_send()
    for d in range(1, 4):
        x_copy(d).wait_send()

    @pl.loop(0, 4)
    def _(i):
        core_copy(i).wait_send()
        for e in range(1, 4):
            y_copy(i, e).wait_send()

        @pl.when((i < 2) & (hands_on | hands_in))
        def _():
            for part in range(2):
                handed_on(lax.rem(i, 2), part).wait_send()

    @pl.loop(0, NC)
    def _(j):
        @pl.when(by_relay(j))
        def _():
            for part in range(2):
                relay_copy(j, part).wait_send()

        @pl.when(jnp.logical_not(by_relay(j)))
        def _():
            ring_copy(j).wait_send()

        own_copy(j).wait_send()
        pair_copy(j).wait_send()

    step_copy.wait_recv()
    diag_ref[...] = tbuf[1] + jnp.where(core == 0, tbuf[2], tbuf[0])

    for copy in z_copies:
        copy.wait_recv()
    total = gsum[z]
    for d in range(7):
        total = total + rz[d]
    dens_ref[...] = total

    step_copy.wait_send()
    for copy in z_copies:
        copy.wait_send()


def hand_over(dens_in_ref, diag_in_ref, dens_ref, diag_ref):
    dens_ref[...] = dens_in_ref[...]
    diag_ref[0] = diag_in_ref[0, 0]


def per_device(cholesky, occ_energy, vir_energy):
    dma = pltpu.SemaphoreType.DMA
    vmem = pltpu.VMEM
    dens, diag = pl.pallas_call(
        kernel,
        out_shape=(jax.ShapeDtypeStruct((8, HALF), f32), jax.ShapeDtypeStruct((8, 128), f32)),
        in_specs=[
            pl.BlockSpec(memory_space=pl.ANY),
            pl.BlockSpec(memory_space=pltpu.SMEM),
            pl.BlockSpec(memory_space=pltpu.VMEM),
        ],
        out_specs=(pl.BlockSpec(memory_space=pltpu.VMEM), pl.BlockSpec(memory_space=pltpu.VMEM)),
        scratch_shapes=[
            vmem((NAUX_HALF, NVIR), bf16),
            vmem((NVIR, NAUX_HALF), bf16),
            vmem((2, NC, NAUX_HALF, CW), bf16),
            vmem((2, NAUX_HALF, CW), bf16),
            vmem((NC, NVIR, CW), bf16),
            vmem((NC, NVIR, CW), bf16),
            vmem((NC, NVIR, CW), f32),
            vmem((2, NVIR, NVIR), bf16),
            vmem((NVIR, NVIR), bf16),
            vmem((16, 4, 2, 8, NVIR), f32),
            vmem((16, 4, 8, NVIR), f32),
            vmem((3, 256, QUARTER), bf16),
            vmem((3, 256, QUARTER), bf16),
            vmem((3, 4, 64, QUARTER), bf16),
            vmem((3, 4, 64, QUARTER), bf16),
            vmem((2, 3, 64, QUARTER), bf16),
            vmem((2, 3, 64, QUARTER), bf16),
            vmem((8, 4, 8, QUARTER), f32),
            vmem((4, 8, 8, QUARTER), f32),
            vmem((8, 8, HALF), f32),
            vmem((7, 8, HALF), f32),
            vmem((3, 8, 128), f32),
            vmem((NVIR, 128), f32),
            dma(()),
            dma((NC,)), dma((NC,)), dma((NC,)), dma((NC,)), dma((NC,)), dma((NC,)),
            dma((2 * NC,)), dma((4,)), dma((4,)), dma((4,)), dma((4,)),
            dma((3,)), dma((3,)), dma((3, 4)), dma((3,)), dma((6,)), dma((6,)), dma((7,)), dma((7,)), dma((2,)), dma((2,)),
        ],
        compiler_params=pltpu.CompilerParams(
            collective_id=0, has_side_effects=True, vmem_limit_bytes=58 * 2**20
        ),
        cost_estimate=pl.CostEstimate(flops=13_000_000_000, bytes_accessed=16_000_000, transcendentals=0),
    )(cholesky, occ_energy, vir_energy.reshape(1, NVIR))
    return pl.pallas_call(
        hand_over,
        out_shape=(jax.ShapeDtypeStruct((8, HALF), f32), jax.ShapeDtypeStruct((1,), f32)),
        in_specs=[pl.BlockSpec(memory_space=pltpu.VMEM), pl.BlockSpec(memory_space=pltpu.VMEM)],
        out_specs=(pl.BlockSpec(memory_space=pltpu.VMEM), pl.BlockSpec(memory_space=pltpu.SMEM)),
    )(dens, diag)


def solution(mesh):
    in_specs = (P("occ", "aux", None), P(), P())
    out_specs = (P("occ", "aux"), P("occ"))
    return jax.shard_map(
        per_device, mesh=mesh, in_specs=in_specs, out_specs=out_specs, check_vma=False
    )
```

```python
import functools

import jax
import jax.numpy as jnp
from jax import lax
from jax.experimental import pallas as pl
from jax.experimental.pallas import tpu as pltpu
from jax.sharding import PartitionSpec as P

MESH = pl.DeviceIdType.MESH
NAUX_HALF = 2560
NVIR = 1024
NOCC = 128
NC = 8
CW = NVIR // NC
LAG = 2
PART = NAUX_HALF // 2
HALF = NVIR // 2
QUARTER = NVIR // 4
f32 = jnp.float32
bf16 = jnp.bfloat16


def kernel(
    x_ref, eocc_ref, v_ref, dens_ref, diag_ref,
    own, own_t, blocks, relay, sendb, recvb, acc, lr, tt, dens, dens_in,
    x_out, x_in, y_out, y_in, second_out, second_in, xsum, ysum, gsum, rz, tbuf, colv,
    own_sem, ys, yr, ds, dr, xs, xr, vs, ls, lw, cs, cr, fs, fr, gs, gr, us, ur, zs, zr, ts, tr,
):
    k = lax.axis_index("occ")
    h = lax.axis_index("aux")
    core = lax.rem(k, 2)
    y = lax.rem(k // 2, 4)
    z = lax.rem(k // 8, 8)
    x = h * 2 + k // 64
    inner = lax.rem(k, 64)

    def x_place(d):
        to = lax.rem(x + d, 4)
        return {"occ": lax.rem(to, 2) * 64 + inner, "aux": to // 2}

    def y_place(d):
        return {"occ": k + (lax.rem(y + d, 4) - y) * 2, "aux": h}

    def z_place(d):
        return {"occ": k + (lax.rem(z + d, 8) - z) * 8, "aux": h}

    above = {"occ": lax.rem(k + 2, NOCC), "aux": h}
    below = {"occ": lax.rem(k + NOCC - 2, NOCC), "aux": h}
    sibling = {"occ": k + 1 - 2 * core, "aux": h}
    partner = {"occ": k, "aux": 1 - h}
    onward = {"occ": lax.rem(k + NOCC - 2 + 4 * core, NOCC), "aux": h}

    up = core == 1
    low = k // 64
    row, level = jnp.where(up, y, 3 - y), jnp.where(up, z, 7 - z)

    def corner_place(low, row, level):
        inner = jnp.where(up, level * 8 + row * 2, (7 - level) * 8 + (3 - row) * 2) + core
        return {"occ": low * 64 + inner, "aux": h}

    def at(row_is, level_is):
        return (row == row_is) & (level == level_is)

    leaves, meets = at(3, 7), at(0, 0)
    early_a, early_b, late_a, late_b = at(3, 4), at(3, 5), at(3, 1), at(3, 2)
    hands_on = early_a | early_b
    hands_in = meets | late_a | late_b
    relay_from = jnp.where(early_a, 1, jnp.where(late_a, 2, jnp.where(late_b, 1, 0)))
    relay_each = jnp.where(meets, 1, 2)

    def remote(src, dst, send, recv, device):
        return pltpu.make_async_remote_copy(
            src_ref=src, dst_ref=dst, send_sem=send, recv_sem=recv, device_id=device, device_id_type=MESH
        )

    load = pltpu.make_async_copy(x_ref.at[0], own, own_sem)
    load.start()

    barrier = pltpu.get_barrier_semaphore()
    greeted = [z_place(d) for d in (4, 3, 5, 2, 6, 1, 7)] + [y_place(d) for d in (2, 1, 3)]
    greeted += [partner, x_place(1), x_place(3), above, below, sibling]
    for device in greeted:
        pl.semaphore_signal(barrier, inc=1, device_id=device, device_id_type=MESH)

    def greet(device):
        pl.semaphore_signal(barrier, inc=1, device_id=device, device_id_type=MESH)

    @pl.when(meets)
    def _():
        greet(corner_place(low, 3, 7))
        greet(corner_place(low, 3, 1))
        greet(corner_place(low, 3, 2))

    @pl.when(hands_on)
    def _():
        greet(corner_place(1 - low, 3, 7))

    @pl.when(late_a | late_b)
    def _():
        greet(corner_place(low, 3, level + 3))

    more = jnp.where(leaves, 3, jnp.where(hands_on | late_a | late_b, 1, 0))
    pl.semaphore_wait(barrier, len(greeted) + more)

    def columns(j):
        return pl.ds(pl.multiple_of(j * CW, CW), CW)

    def ring_copy(j):
        return remote(x_ref.at[0, :, columns(j)], blocks.at[0, j], ys.at[j], yr.at[j], onward)

    def relay_copy(j, part):
        place = corner_place(
            jnp.where(j < 4, low, 1 - low), jnp.where(j < 4, 0, 3), jnp.where(j < 4, 0, 5 - lax.rem(j, 2))
        )
        slot = jnp.where(j < 4, lax.rem(j, 2), lax.rem(j // 2, 2))
        rows = pl.ds(part * PART, PART)
        return remote(
            x_ref.at[0, rows, columns(j)], relay.at[slot, rows], vs.at[2 * j + part], lw.at[2 * slot + part], place
        )

    def handed_on(i, part):
        here = relay.at[i, pl.ds(part * PART, PART)]
        place = corner_place(low, 3, jnp.where(hands_on, level - 3, level))
        return remote(here, here, ls.at[2 * i + part], lw.at[2 * i + part], place)

    def handed_in(i, part):
        j = jnp.where(meets, i, 2 * i + jnp.where(late_a, 5, 4))
        place = corner_place(jnp.where(meets, 1 - low, low), 0, 0)
        rows = pl.ds(part * PART, PART)
        return remote(relay.at[i, rows], blocks.at[0, j, rows], ls.at[2 * i + part], yr.at[j], place)

    def by_relay(j):
        return leaves & ((j >= 4) | (j < 2))

    def own_copy(j):
        return remote(x_ref.at[0, :, columns(j)], blocks.at[1, j], ds.at[j], dr.at[j], sibling)

    def pass_copy(j):
        return remote(blocks.at[0, j], blocks.at[1, j], ds.at[j], dr.at[j], sibling)

    def pair_copy(j):
        return remote(sendb.at[j], recvb.at[j], xs.at[j], xr.at[j], partner)

    @pl.loop(0, NC)
    def _(j):
        @pl.when(by_relay(j))
        def _():
            for part in range(2):
                relay_copy(j, part).start()

        @pl.when(jnp.logical_not(by_relay(j)))
        def _():
            ring_copy(j).start()

        @pl.when(core == 0)
        def _():
            own_copy(j).start()

    for m in range(8):
        row = v_ref[0:1, m * 128:(m + 1) * 128]
        colv[m * 128:(m + 1) * 128, :] = jnp.broadcast_to(row, (128, 128)).T

    load.wait()

    @pl.loop(0, NAUX_HALF // 128)
    def _(i):
        rows = pl.ds(pl.multiple_of(i * 128, 128), 128)
        own_t[:, rows] = own[rows, :].T

    center = lax.rem(k - h - 2 * core * (1 - h) + NOCC, NOCC)
    other = lax.rem(center + 2 - h, NOCC)
    center_energy = eocc_ref[center]
    other_energy = eocc_ref[other]
    place = 1 - (1 - core) * (1 - h)

    def finish(j):
        pair_copy(j).wait_recv()
        vrow = v_ref[0:1, columns(j)]

        for m in range(8):
            rows = pl.ds(m * 128, 128)
            total = acc[j, rows, :] + recvb[j, rows, :].astype(f32)
            part = total / (colv[rows, :] + vrow - center_energy - other_energy)
            lr[place, rows, columns(j)] = part.astype(bf16)
            lr[1 - place, columns(j), rows] = part.T.astype(bf16)

        strip = columns(j)
        tt[strip, :] = (2.0 * lr[1, strip, :].astype(f32) - lr[0, strip, :].astype(f32)).astype(bf16)
        tt[:, strip] = (2.0 * lr[1, :, strip].astype(f32) - lr[0, :, strip].astype(f32)).astype(bf16)

    def product(stream, j):
        @pl.when(stream == 0)
        def _():
            ring_copy(j).wait_recv()

            @pl.when(up)
            def _():
                pass_copy(j).start()

        @pl.when(stream == 1)
        def _():
            own_copy(j).wait_recv()

        @pl.when(stream == h)
        def _():
            for m in range(4):
                rows = pl.ds(m * 256, 256)
                acc[j, rows, :] = jnp.dot(own_t[rows, :], blocks[stream, j], preferred_element_type=f32)

        @pl.when(stream != h)
        def _():
            for m in range(4):
                rows = pl.ds(m * 256, 256)
                sendb[j, rows, :] = jnp.dot(
                    own_t[rows, :], blocks[stream, j], preferred_element_type=f32
                ).astype(bf16)
            pair_copy(j).start()

    late_ring = meets
    late_passed = (core == 0) & (y == 0) & (z == 0)
    lag = jnp.where(late_ring | late_passed, LAG, 0)
    sooner = jnp.where(late_ring, 1, jnp.where(late_passed, 0, 1 - h))

    @pl.loop(0, NC + LAG + 1)
    def _(j):
        @pl.loop(0, 3)
        def _(q):
            early = up & (q < 2)
            stream = jnp.where(up, jnp.where(early, 1, 0), jnp.where(q == 0, sooner, 1 - sooner))
            turn = jnp.where(early, 2 * j + q, jnp.where(q == 0, j, j - lag))

            @pl.when((turn >= 0) & (turn < NC) & (up | (q < 2)))
            def _():
                product(stream, turn)

        since = j - relay_from
        slot = jnp.where(since == 0, 0, 1)

        @pl.when((hands_on | hands_in) & ((since == 0) | (since == relay_each)))
        def _():
            for part in range(2):
                handed_on(slot, part).wait_recv()

                @pl.when(hands_on)
                def _():
                    handed_on(slot, part).start()

                @pl.when(hands_in)
                def _():
                    handed_in(slot, part).start()

        done = j - 1 - lag

        @pl.when((done >= 0) & (done < NC))
        def _():
            finish(done)

    def term_rows(i, term):
        rows = pl.ds(pl.multiple_of(i * 128, 128), 128)
        product = lr[1, rows, :].astype(f32) * tt[rows, :].astype(f32)
        return term + jnp.sum(product.reshape(16, 8, 8, 128), axis=(0, 2))

    def quadrant(q):
        d = jnp.where(q == 0, 2, jnp.where(q == 1, 1, jnp.where(q == 2, 3, 0)))
        to = lax.rem(x + d, 4)
        return d, to, lax.rem(to, 2), to // 2

    def core_copy(q):
        _, _, upper, side = quadrant(q)
        rows = pl.ds(upper * 8, 8)
        cols = pl.ds(pl.multiple_of(side * HALF, HALF), HALF)
        return remote(
            dens.at[rows, :, 1 - core, :, cols], dens_in.at[rows, :, :, cols], cs.at[q], cr.at[q], sibling
        )

    def x_copy(d):
        return remote(x_out.at[d - 1], x_in.at[d - 1], fs.at[d - 1], fr.at[d - 1], x_place(d))

    def y_copy(to, e):
        return remote(y_out.at[e - 1, to], y_in.at[e - 1, to], gs.at[e - 1, to], gr.at[e - 1], y_place(e))

    @pl.loop(0, 5)
    def _(q):
        @pl.when(q < 4)
        def _():
            _, _, upper, side = quadrant(q)
            rows = pl.ds(pl.multiple_of(upper * HALF, HALF), HALF)
            cols = pl.ds(pl.multiple_of(side * HALF, HALF), HALF)
            out = 2.0 * jnp.dot(lr[0, rows, :], tt[:, cols], preferred_element_type=f32)
            dens[pl.ds(upper * 8, 8), :, :, :, cols] = out.reshape(8, 4, 2, 8, HALF)
            core_copy(q).start()

        @pl.when(q > 0)
        def _():
            core_copy(q - 1).wait_recv()
            d, to, upper, side = quadrant(q - 1)
            rows = pl.ds(upper * 8, 8)
            left = pl.ds(pl.multiple_of(side * HALF, QUARTER), QUARTER)
            right = pl.ds(pl.multiple_of(side * HALF + QUARTER, QUARTER), QUARTER)
            part = dens[rows, :, core, :, left] + dens_in[rows, :, :, left]

            @pl.when(d == 0)
            def _():
                xsum[...] = part

            @pl.when(d > 0)
            def _():
                away = jnp.maximum(d, 1)
                x_out[away - 1] = part.reshape(256, QUARTER).astype(bf16)
                x_copy(away).start()

            for e in (2, 1, 3, 0):
                row = lax.rem(y + e, 4)
                part = dens[rows, row, core, :, right] + dens_in[rows, row, :, right]
                if e == 0:
                    ysum[to] = part
                else:
                    y_out[e - 1, to] = part.reshape(64, QUARTER).astype(bf16)
                    y_copy(to, e).start()

    term = lax.fori_loop(0, 8, term_rows, jnp.zeros((8, 128), f32))
    tbuf[h] = jnp.full((8, 128), -(2.0 / NVIR) * jnp.sum(term), f32)
    term_copy = remote(tbuf.at[h], tbuf.at[h], ts.at[0], tr.at[0], partner)
    term_copy.start()

    for d in (1, 3, 2):
        x_copy(d).wait_recv()
        xsum[...] += x_in[d - 1].astype(f32).reshape(8, 4, 8, QUARTER)
        remote(y_out.at[d - 1], y_in.at[d - 1], gs.at[d - 1, 0], gr.at[d - 1], y_place(d)).wait_recv()
        ysum[...] += y_in[d - 1].astype(f32).reshape(4, 8, 8, QUARTER)

    def second_copy(way, d):
        i = way * 3 + d - 1
        to = x_place(d) if way else y_place(d)
        return remote(second_out.at[way, d - 1], second_in.at[way, d - 1], us.at[i], ur.at[i], to)

    for d in (2, 1, 3):
        second_out[0, d - 1] = xsum[:, lax.rem(y + d, 4)].reshape(64, QUARTER).astype(bf16)
        second_copy(0, d).start()
        second_out[1, d - 1] = ysum[lax.rem(x + d, 4)].reshape(64, QUARTER).astype(bf16)
        second_copy(1, d).start()
    term_copy.wait()
    step_copy = remote(tbuf.at[0], tbuf.at[2], ts.at[1], tr.at[1], above)
    step_copy.start()

    left, right = xsum[:, y], ysum[x]
    for d in (1, 3, 2):
        second_copy(0, d).wait_recv()
        left = left + second_in[0, d - 1].astype(f32).reshape(8, 8, QUARTER)
        second_copy(1, d).wait_recv()
        right = right + second_in[1, d - 1].astype(f32).reshape(8, 8, QUARTER)
    gsum[:, :, :QUARTER] = left
    gsum[:, :, QUARTER:] = right

    z_copies = []
    for d in (4, 3, 5, 2, 6, 1, 7):
        copy = remote(gsum.at[lax.rem(z + d, 8)], rz.at[d - 1], zs.at[d - 1], zr.at[d - 1], z_place(d))
        copy.start()
        z_copies.append(copy)

    for way in range(2):
        for d in range(1, 4):
            second_copy(way, d).wait_send()
    for d in range(1, 4):
        x_copy(d).wait_send()

    @pl.loop(0, 4)
    def _(i):
        core_copy(i).wait_send()
        for e in range(1, 4):
            y_copy(i, e).wait_send()

        @pl.when((i < 2) & (hands_on | hands_in))
        def _():
            for part in range(2):
                handed_on(lax.rem(i, 2), part).wait_send()

    @pl.loop(0, NC)
    def _(j):
        @pl.when(by_relay(j))
        def _():
            for part in range(2):
                relay_copy(j, part).wait_send()

        @pl.when(jnp.logical_not(by_relay(j)))
        def _():
            ring_copy(j).wait_send()

        own_copy(j).wait_send()
        pair_copy(j).wait_send()

    step_copy.wait_recv()
    diag_ref[...] = tbuf[1] + jnp.where(core == 0, tbuf[2], tbuf[0])

    for copy in z_copies:
        copy.wait_recv()
    total = gsum[z]
    for d in range(7):
        total = total + rz[d]
    dens_ref[...] = total

    step_copy.wait_send()
    for copy in z_copies:
        copy.wait_send()


def hand_over(dens_in_ref, diag_in_ref, dens_ref, diag_ref):
    dens_ref[...] = dens_in_ref[...]
    diag_ref[0] = diag_in_ref[0, 0]


def per_device(cholesky, occ_energy, vir_energy):
    dma = pltpu.SemaphoreType.DMA
    vmem = pltpu.VMEM
    dens, diag = pl.pallas_call(
        kernel,
        out_shape=(jax.ShapeDtypeStruct((8, HALF), f32), jax.ShapeDtypeStruct((8, 128), f32)),
        in_specs=[
            pl.BlockSpec(memory_space=pl.ANY),
            pl.BlockSpec(memory_space=pltpu.SMEM),
            pl.BlockSpec(memory_space=pltpu.VMEM),
        ],
        out_specs=(pl.BlockSpec(memory_space=pltpu.VMEM), pl.BlockSpec(memory_space=pltpu.VMEM)),
        scratch_shapes=[
            vmem((NAUX_HALF, NVIR), bf16),
            vmem((NVIR, NAUX_HALF), bf16),
            vmem((2, NC, NAUX_HALF, CW), bf16),
            vmem((2, NAUX_HALF, CW), bf16),
            vmem((NC, NVIR, CW), bf16),
            vmem((NC, NVIR, CW), bf16),
            vmem((NC, NVIR, CW), f32),
            vmem((2, NVIR, NVIR), bf16),
            vmem((NVIR, NVIR), bf16),
            vmem((16, 4, 2, 8, NVIR), f32),
            vmem((16, 4, 8, NVIR), f32),
            vmem((3, 256, QUARTER), bf16),
            vmem((3, 256, QUARTER), bf16),
            vmem((3, 4, 64, QUARTER), bf16),
            vmem((3, 4, 64, QUARTER), bf16),
            vmem((2, 3, 64, QUARTER), bf16),
            vmem((2, 3, 64, QUARTER), bf16),
            vmem((8, 4, 8, QUARTER), f32),
            vmem((4, 8, 8, QUARTER), f32),
            vmem((8, 8, HALF), f32),
            vmem((7, 8, HALF), f32),
            vmem((3, 8, 128), f32),
            vmem((NVIR, 128), f32),
            dma(()),
            dma((NC,)), dma((NC,)), dma((NC,)), dma((NC,)), dma((NC,)), dma((NC,)),
            dma((2 * NC,)), dma((4,)), dma((4,)), dma((4,)), dma((4,)),
            dma((3,)), dma((3,)), dma((3, 4)), dma((3,)), dma((6,)), dma((6,)), dma((7,)), dma((7,)), dma((2,)), dma((2,)),
        ],
        compiler_params=pltpu.CompilerParams(
            collective_id=0, has_side_effects=True, vmem_limit_bytes=58 * 2**20
        ),
        cost_estimate=pl.CostEstimate(flops=13_000_000_000, bytes_accessed=16_000_000, transcendentals=0),
    )(cholesky, occ_energy, vir_energy.reshape(1, NVIR))
    return pl.pallas_call(
        hand_over,
        out_shape=(jax.ShapeDtypeStruct((8, HALF), f32), jax.ShapeDtypeStruct((1,), f32)),
        in_specs=[pl.BlockSpec(memory_space=pltpu.VMEM), pl.BlockSpec(memory_space=pltpu.VMEM)],
        out_specs=(pl.BlockSpec(memory_space=pltpu.VMEM), pl.BlockSpec(memory_space=pltpu.SMEM)),
    )(dens, diag)


def solution(mesh):
    in_specs = (P("occ", "aux", None), P(), P())
    out_specs = (P("occ", "aux"), P("occ"))
    return jax.shard_map(
        per_device, mesh=mesh, in_specs=in_specs, out_specs=out_specs, check_vma=False
    )
```

```python
import functools

import jax
import jax.numpy as jnp
from jax import lax
from jax.experimental import pallas as pl
from jax.experimental.pallas import tpu as pltpu
from jax.sharding import PartitionSpec as P

MESH = pl.DeviceIdType.MESH
NAUX_HALF = 2560
NVIR = 1024
NOCC = 128
NC = 8
CW = NVIR // NC
LAG = 2
PART = NAUX_HALF // 2
HALF = NVIR // 2
QUARTER = NVIR // 4
f32 = jnp.float32
bf16 = jnp.bfloat16


def kernel(
    x_ref, eocc_ref, v_ref, dens_ref, diag_ref,
    own, own_t, blocks, relay, sendb, recvb, acc, lr, tt, dens, dens_in,
    x_out, x_in, y_out, y_in, second_out, second_in, xsum, ysum, gsum, rz, tbuf, colv,
    own_sem, ys, yr, ds, dr, xs, xr, vs, ls, lw, cs, cr, fs, fr, gs, gr, us, ur, zs, zr, ts, tr,
):
    k = lax.axis_index("occ")
    h = lax.axis_index("aux")
    core = lax.rem(k, 2)
    y = lax.rem(k // 2, 4)
    z = lax.rem(k // 8, 8)
    x = h * 2 + k // 64
    inner = lax.rem(k, 64)

    def x_place(d):
        to = lax.rem(x + d, 4)
        return {"occ": lax.rem(to, 2) * 64 + inner, "aux": to // 2}

    def y_place(d):
        return {"occ": k + (lax.rem(y + d, 4) - y) * 2, "aux": h}

    def z_place(d):
        return {"occ": k + (lax.rem(z + d, 8) - z) * 8, "aux": h}

    above = {"occ": lax.rem(k + 2, NOCC), "aux": h}
    below = {"occ": lax.rem(k + NOCC - 2, NOCC), "aux": h}
    sibling = {"occ": k + 1 - 2 * core, "aux": h}
    partner = {"occ": k, "aux": 1 - h}
    onward = {"occ": lax.rem(k + NOCC - 2 + 4 * core, NOCC), "aux": h}

    up = core == 1
    low = k // 64
    row, level = jnp.where(up, y, 3 - y), jnp.where(up, z, 7 - z)

    def corner_place(low, row, level):
        inner = jnp.where(up, level * 8 + row * 2, (7 - level) * 8 + (3 - row) * 2) + core
        return {"occ": low * 64 + inner, "aux": h}

    def at(row_is, level_is):
        return (row == row_is) & (level == level_is)

    leaves, meets = at(3, 7), at(0, 0)
    early_a, early_b, late_a, late_b = at(3, 4), at(3, 5), at(3, 1), at(3, 2)
    hands_on = early_a | early_b
    hands_in = meets | late_a | late_b
    relay_from = jnp.where(early_a, 1, jnp.where(late_a, 2, jnp.where(late_b, 1, 0)))
    relay_each = jnp.where(meets, 1, 2)

    def remote(src, dst, send, recv, device):
        return pltpu.make_async_remote_copy(
            src_ref=src, dst_ref=dst, send_sem=send, recv_sem=recv, device_id=device, device_id_type=MESH
        )

    load = pltpu.make_async_copy(x_ref.at[0], own, own_sem)
    load.start()

    barrier = pltpu.get_barrier_semaphore()
    greeted = [z_place(d) for d in (4, 3, 5, 2, 6, 1, 7)] + [y_place(d) for d in (2, 1, 3)]
    greeted += [partner, x_place(1), x_place(3), above, below, sibling]
    for device in greeted:
        pl.semaphore_signal(barrier, inc=1, device_id=device, device_id_type=MESH)

    def greet(device):
        pl.semaphore_signal(barrier, inc=1, device_id=device, device_id_type=MESH)

    @pl.when(meets)
    def _():
        greet(corner_place(low, 3, 7))
        greet(corner_place(low, 3, 1))
        greet(corner_place(low, 3, 2))

    @pl.when(hands_on)
    def _():
        greet(corner_place(1 - low, 3, 7))

    @pl.when(late_a | late_b)
    def _():
        greet(corner_place(low, 3, level + 3))

    more = jnp.where(leaves, 3, jnp.where(hands_on | late_a | late_b, 1, 0))
    pl.semaphore_wait(barrier, len(greeted) + more)

    def columns(j):
        return pl.ds(pl.multiple_of(j * CW, CW), CW)

    def ring_copy(j):
        return remote(x_ref.at[0, :, columns(j)], blocks.at[0, j], ys.at[j], yr.at[j], onward)

    def relay_copy(j, part):
        place = corner_place(
            jnp.where(j < 4, low, 1 - low), jnp.where(j < 4, 0, 3), jnp.where(j < 4, 0, 5 - lax.rem(j, 2))
        )
        slot = jnp.where(j < 4, lax.rem(j, 2), lax.rem(j // 2, 2))
        rows = pl.ds(part * PART, PART)
        return remote(
            x_ref.at[0, rows, columns(j)], relay.at[slot, rows], vs.at[2 * j + part], lw.at[2 * slot + part], place
        )

    def handed_on(i, part):
        here = relay.at[i, pl.ds(part * PART, PART)]
        place = corner_place(low, 3, jnp.where(hands_on, level - 3, level))
        return remote(here, here, ls.at[2 * i + part], lw.at[2 * i + part], place)

    def handed_in(i, part):
        j = jnp.where(meets, i, 2 * i + jnp.where(late_a, 5, 4))
        place = corner_place(jnp.where(meets, 1 - low, low), 0, 0)
        rows = pl.ds(part * PART, PART)
        return remote(relay.at[i, rows], blocks.at[0, j, rows], ls.at[2 * i + part], yr.at[j], place)

    def by_relay(j):
        return leaves & ((j >= 4) | (j < 2))

    def own_copy(j):
        return remote(x_ref.at[0, :, columns(j)], blocks.at[1, j], ds.at[j], dr.at[j], sibling)

    def pass_copy(j):
        return remote(blocks.at[0, j], blocks.at[1, j], ds.at[j], dr.at[j], sibling)

    def pair_copy(j):
        return remote(sendb.at[j], recvb.at[j], xs.at[j], xr.at[j], partner)

    @pl.loop(0, NC)
    def _(j):
        @pl.when(by_relay(j))
        def _():
            for part in range(2):
                relay_copy(j, part).start()

        @pl.when(jnp.logical_not(by_relay(j)))
        def _():
            ring_copy(j).start()

        @pl.when(core == 0)
        def _():
            own_copy(j).start()

    for m in range(8):
        row = v_ref[0:1, m * 128:(m + 1) * 128]
        colv[m * 128:(m + 1) * 128, :] = jnp.broadcast_to(row, (128, 128)).T

    load.wait()

    @pl.loop(0, NAUX_HALF // 128)
    def _(i):
        rows = pl.ds(pl.multiple_of(i * 128, 128), 128)
        own_t[:, rows] = own[rows, :].T

    center = lax.rem(k - h - 2 * core * (1 - h) + NOCC, NOCC)
    other = lax.rem(center + 2 - h, NOCC)
    center_energy = eocc_ref[center]
    other_energy = eocc_ref[other]
    place = 1 - (1 - core) * (1 - h)

    def finish(j):
        pair_copy(j).wait_recv()
        vrow = v_ref[0:1, columns(j)]

        for m in range(8):
            rows = pl.ds(m * 128, 128)
            total = acc[j, rows, :] + recvb[j, rows, :].astype(f32)
            part = total / (colv[rows, :] + vrow - center_energy - other_energy)
            lr[place, rows, columns(j)] = part.astype(bf16)
            lr[1 - place, columns(j), rows] = part.T.astype(bf16)

        strip = columns(j)
        tt[strip, :] = (2.0 * lr[1, strip, :].astype(f32) - lr[0, strip, :].astype(f32)).astype(bf16)
        tt[:, strip] = (2.0 * lr[1, :, strip].astype(f32) - lr[0, :, strip].astype(f32)).astype(bf16)

    def product(stream, j):
        @pl.when(stream == 0)
        def _():
            ring_copy(j).wait_recv()

            @pl.when(up)
            def _():
                pass_copy(j).start()

        @pl.when(stream == 1)
        def _():
            own_copy(j).wait_recv()

        @pl.when(stream == h)
        def _():
            for m in range(4):
                rows = pl.ds(m * 256, 256)
                acc[j, rows, :] = jnp.dot(own_t[rows, :], blocks[stream, j], preferred_element_type=f32)

        @pl.when(stream != h)
        def _():
            for m in range(4):
                rows = pl.ds(m * 256, 256)
                sendb[j, rows, :] = jnp.dot(
                    own_t[rows, :], blocks[stream, j], preferred_element_type=f32
                ).astype(bf16)
            pair_copy(j).start()

    late_ring = meets
    late_passed = (core == 0) & (y == 0) & (z == 0)
    lag = jnp.where(late_ring | late_passed, LAG, 0)
    sooner = jnp.where(late_ring, 1, jnp.where(late_passed, 0, 1 - h))

    @pl.loop(0, NC + LAG + 1)
    def _(j):
        @pl.loop(0, 3)
        def _(q):
            early = up & (q < 2)
            stream = jnp.where(up, jnp.where(early, 1, 0), jnp.where(q == 0, sooner, 1 - sooner))
            turn = jnp.where(early, 2 * j + q, jnp.where(q == 0, j, j - lag))

            @pl.when((turn >= 0) & (turn < NC) & (up | (q < 2)))
            def _():
                product(stream, turn)

        since = j - relay_from
        slot = jnp.where(since == 0, 0, 1)

        @pl.when((hands_on | hands_in) & ((since == 0) | (since == relay_each)))
        def _():
            for part in range(2):
                handed_on(slot, part).wait_recv()

                @pl.when(hands_on)
                def _():
                    handed_on(slot, part).start()

                @pl.when(hands_in)
                def _():
                    handed_in(slot, part).start()

        done = j - 1 - lag

        @pl.when((done >= 0) & (done < NC))
        def _():
            finish(done)

    def term_rows(i, term):
        rows = pl.ds(pl.multiple_of(i * 128, 128), 128)
        product = lr[1, rows, :].astype(f32) * tt[rows, :].astype(f32)
        return term + jnp.sum(product.reshape(16, 8, 8, 128), axis=(0, 2))

    def quadrant(q):
        d = jnp.where(q == 0, 2, jnp.where(q == 1, 1, jnp.where(q == 2, 3, 0)))
        to = lax.rem(x + d, 4)
        return d, to, lax.rem(to, 2), to // 2

    def core_copy(q):
        _, _, upper, side = quadrant(q)
        rows = pl.ds(upper * 8, 8)
        cols = pl.ds(pl.multiple_of(side * HALF, HALF), HALF)
        return remote(
            dens.at[rows, :, 1 - core, :, cols], dens_in.at[rows, :, :, cols], cs.at[q], cr.at[q], sibling
        )

    def x_copy(d):
        return remote(x_out.at[d - 1], x_in.at[d - 1], fs.at[d - 1], fr.at[d - 1], x_place(d))

    def y_copy(to, e):
        return remote(y_out.at[e - 1, to], y_in.at[e - 1, to], gs.at[e - 1, to], gr.at[e - 1], y_place(e))

    @pl.loop(0, 5)
    def _(q):
        @pl.when(q < 4)
        def _():
            _, _, upper, side = quadrant(q)
            rows = pl.ds(pl.multiple_of(upper * HALF, HALF), HALF)
            cols = pl.ds(pl.multiple_of(side * HALF, HALF), HALF)
            out = jnp.dot(lr[0, rows, :], tt[:, cols], preferred_element_type=f32)
            dens[pl.ds(upper * 8, 8), :, :, :, cols] = out.reshape(8, 4, 2, 8, HALF)
            core_copy(q).start()

        @pl.when(q > 0)
        def _():
            core_copy(q - 1).wait_recv()
            d, to, upper, side = quadrant(q - 1)
            rows = pl.ds(upper * 8, 8)
            left = pl.ds(pl.multiple_of(side * HALF, QUARTER), QUARTER)
            right = pl.ds(pl.multiple_of(side * HALF + QUARTER, QUARTER), QUARTER)
            part = dens[rows, :, core, :, left] + dens_in[rows, :, :, left]

            @pl.when(d == 0)
            def _():
                xsum[...] = part

            @pl.when(d > 0)
            def _():
                away = jnp.maximum(d, 1)
                x_out[away - 1] = part.reshape(256, QUARTER).astype(bf16)
                x_copy(away).start()

            for e in (2, 1, 3, 0):
                row = lax.rem(y + e, 4)
                part = dens[rows, row, core, :, right] + dens_in[rows, row, :, right]
                if e == 0:
                    ysum[to] = part
                else:
                    y_out[e - 1, to] = part.reshape(64, QUARTER).astype(bf16)
                    y_copy(to, e).start()

    term = lax.fori_loop(0, 8, term_rows, jnp.zeros((8, 128), f32))
    tbuf[h] = jnp.full((8, 128), -(2.0 / NVIR) * jnp.sum(term), f32)
    term_copy = remote(tbuf.at[h], tbuf.at[h], ts.at[0], tr.at[0], partner)
    term_copy.start()

    for d in (1, 3, 2):
        x_copy(d).wait_recv()
        xsum[...] += x_in[d - 1].astype(f32).reshape(8, 4, 8, QUARTER)
        remote(y_out.at[d - 1], y_in.at[d - 1], gs.at[d - 1, 0], gr.at[d - 1], y_place(d)).wait_recv()
        ysum[...] += y_in[d - 1].astype(f32).reshape(4, 8, 8, QUARTER)

    def second_copy(way, d):
        i = way * 3 + d - 1
        to = x_place(d) if way else y_place(d)
        return remote(second_out.at[way, d - 1], second_in.at[way, d - 1], us.at[i], ur.at[i], to)

    for d in (2, 1, 3):
        second_out[0, d - 1] = xsum[:, lax.rem(y + d, 4)].reshape(64, QUARTER).astype(bf16)
        second_copy(0, d).start()
        second_out[1, d - 1] = ysum[lax.rem(x + d, 4)].reshape(64, QUARTER).astype(bf16)
        second_copy(1, d).start()
    term_copy.wait()
    step_copy = remote(tbuf.at[0], tbuf.at[2], ts.at[1], tr.at[1], above)
    step_copy.start()

    left, right = xsum[:, y], ysum[x]
    for d in (1, 3, 2):
        second_copy(0, d).wait_recv()
        left = left + second_in[0, d - 1].astype(f32).reshape(8, 8, QUARTER)
        second_copy(1, d).wait_recv()
        right = right + second_in[1, d - 1].astype(f32).reshape(8, 8, QUARTER)
    gsum[:, :, :QUARTER] = left
    gsum[:, :, QUARTER:] = right

    z_copies = []
    for d in (4, 3, 5, 2, 6, 1, 7):
        copy = remote(gsum.at[lax.rem(z + d, 8)], rz.at[d - 1], zs.at[d - 1], zr.at[d - 1], z_place(d))
        copy.start()
        z_copies.append(copy)

    for way in range(2):
        for d in range(1, 4):
            second_copy(way, d).wait_send()
    for d in range(1, 4):
        x_copy(d).wait_send()

    @pl.loop(0, 4)
    def _(i):
        core_copy(i).wait_send()
        for e in range(1, 4):
            y_copy(i, e).wait_send()

        @pl.when((i < 2) & (hands_on | hands_in))
        def _():
            for part in range(2):
                handed_on(lax.rem(i, 2), part).wait_send()

    @pl.loop(0, NC)
    def _(j):
        @pl.when(by_relay(j))
        def _():
            for part in range(2):
                relay_copy(j, part).wait_send()

        @pl.when(jnp.logical_not(by_relay(j)))
        def _():
            ring_copy(j).wait_send()

        own_copy(j).wait_send()
        pair_copy(j).wait_send()

    step_copy.wait_recv()
    diag_ref[...] = tbuf[1] + jnp.where(core == 0, tbuf[2], tbuf[0])

    for copy in z_copies:
        copy.wait_recv()
    total = gsum[z]
    for d in range(7):
        total = total + rz[d]
    dens_ref[...] = 2.0 * total

    step_copy.wait_send()
    for copy in z_copies:
        copy.wait_send()


def hand_over(dens_in_ref, diag_in_ref, dens_ref, diag_ref):
    dens_ref[...] = dens_in_ref[...]
    diag_ref[0] = diag_in_ref[0, 0]


def per_device(cholesky, occ_energy, vir_energy):
    dma = pltpu.SemaphoreType.DMA
    vmem = pltpu.VMEM
    dens, diag = pl.pallas_call(
        kernel,
        out_shape=(jax.ShapeDtypeStruct((8, HALF), f32), jax.ShapeDtypeStruct((8, 128), f32)),
        in_specs=[
            pl.BlockSpec(memory_space=pl.ANY),
            pl.BlockSpec(memory_space=pltpu.SMEM),
            pl.BlockSpec(memory_space=pltpu.VMEM),
        ],
        out_specs=(pl.BlockSpec(memory_space=pltpu.VMEM), pl.BlockSpec(memory_space=pltpu.VMEM)),
        scratch_shapes=[
            vmem((NAUX_HALF, NVIR), bf16),
            vmem((NVIR, NAUX_HALF), bf16),
            vmem((2, NC, NAUX_HALF, CW), bf16),
            vmem((2, NAUX_HALF, CW), bf16),
            vmem((NC, NVIR, CW), bf16),
            vmem((NC, NVIR, CW), bf16),
            vmem((NC, NVIR, CW), f32),
            vmem((2, NVIR, NVIR), bf16),
            vmem((NVIR, NVIR), bf16),
            vmem((16, 4, 2, 8, NVIR), f32),
            vmem((16, 4, 8, NVIR), f32),
            vmem((3, 256, QUARTER), bf16),
            vmem((3, 256, QUARTER), bf16),
            vmem((3, 4, 64, QUARTER), bf16),
            vmem((3, 4, 64, QUARTER), bf16),
            vmem((2, 3, 64, QUARTER), bf16),
            vmem((2, 3, 64, QUARTER), bf16),
            vmem((8, 4, 8, QUARTER), f32),
            vmem((4, 8, 8, QUARTER), f32),
            vmem((8, 8, HALF), f32),
            vmem((7, 8, HALF), f32),
            vmem((3, 8, 128), f32),
            vmem((NVIR, 128), f32),
            dma(()),
            dma((NC,)), dma((NC,)), dma((NC,)), dma((NC,)), dma((NC,)), dma((NC,)),
            dma((2 * NC,)), dma((4,)), dma((4,)), dma((4,)), dma((4,)),
            dma((3,)), dma((3,)), dma((3, 4)), dma((3,)), dma((6,)), dma((6,)), dma((7,)), dma((7,)), dma((2,)), dma((2,)),
        ],
        compiler_params=pltpu.CompilerParams(
            collective_id=0, has_side_effects=True, vmem_limit_bytes=58 * 2**20
        ),
        cost_estimate=pl.CostEstimate(flops=13_000_000_000, bytes_accessed=16_000_000, transcendentals=0),
    )(cholesky, occ_energy, vir_energy.reshape(1, NVIR))
    return pl.pallas_call(
        hand_over,
        out_shape=(jax.ShapeDtypeStruct((8, HALF), f32), jax.ShapeDtypeStruct((1,), f32)),
        in_specs=[pl.BlockSpec(memory_space=pltpu.VMEM), pl.BlockSpec(memory_space=pltpu.VMEM)],
        out_specs=(pl.BlockSpec(memory_space=pltpu.VMEM), pl.BlockSpec(memory_space=pltpu.SMEM)),
    )(dens, diag)


def solution(mesh):
    in_specs = (P("occ", "aux", None), P(), P())
    out_specs = (P("occ", "aux"), P("occ"))
    return jax.shard_map(
        per_device, mesh=mesh, in_specs=in_specs, out_specs=out_specs, check_vma=False
    )
```
